32 devices in a mesh: dp: 16 (over z, y, x), tensor: 2 (over core).
Axes of the slice: x: 2, y: 2, z: 4, core: 2. Of those that a mesh axis runs over, the one named last changes fastest.
Arguments:
- block_input_tokens: float32 [6304, 768], P(('dp', 'tensor')), may hold values from -6 to 6
- weights: float32 [12, 768, 768], P(None, 'dp', 'tensor'), may hold values from -2.4537386 to 2.4537386
- vectors: float32 [12, 768], replicated, may hold values from -0.5 to 1.5
- momentum: float32 [12, 768, 768], P(None, 'dp', 'tensor'), may hold values from -128 to 128
- adam_first: float32 [12, 768], replicated, may hold values from -48 to 48
- adam_second: float32 [12, 768], replicated, may hold values from 63.04 to 630.4
- output_gradient: float32 [6304, 768], P(('dp', 'tensor')), may hold values from -6 to 6
Outputs:
- output: float32 [6304, 768], P(('dp', 'tensor'))
- input_gradient: float32 [6304, 768], P(('dp', 'tensor'))
- weight_grad: float32 [12, 768, 768], P(None, 'dp', 'tensor')
- new_weights: float32 [12, 768, 768], P(None, 'dp', 'tensor')
- new_momentum: float32 [12, 768, 768], P(None, 'dp', 'tensor')
- vector_grad: float32 [12, 768], replicated
- new_vectors: float32 [12, 768], replicated
- new_adam_first: float32 [12, 768], replicated
- new_adam_second: float32 [12, 768], replicated
The draws below stay inside these ranges and needn't reach their ends.
All inputs are finite; a program needn't handle non-finite values.
Results may differ from the reference program's by a relative error of at most 0.013.
Values may be sent and summed in bfloat16 or wider, within the bound.
No kernel may reach another device: no remote copies, remote signals or barrier semaphores. Data moves between devices by JAX's collectives and lax.ppermute only.
A program may use at most 192 MiB of HBM per device.

```python
import math
import jax
import jax.numpy as jnp
from jax import lax

D = 768
HEADS = 12
HDIM = 64
FF = 3072
SEQ = 197
NS_STEPS = 5
NBLK = 12
NVEC = 12
IMAGES = 32
TOKENS = 6304
N_TENSOR = 2


def draw_block_input_tokens(key, part):
    first = jax.random.fold_in(key, 11)
    return jax.random.truncated_normal(first, -6.0, 6.0, (TOKENS, D), jnp.float32)


def draw_weights(key, part):
    first = jax.random.fold_in(key, 23)
    count = FF // D
    raw = jax.random.truncated_normal(first, -3.0, 3.0, (4 + 2 * count, D, D), jnp.float32)
    factor = jnp.concatenate([jnp.full((3,), D ** (-0.5), jnp.float32), jnp.full((1,), 3.0 * D ** (-0.5), jnp.float32), jnp.full((count,), D ** (-0.5), jnp.float32), jnp.full((count,), FF ** (-0.5), jnp.float32)])
    return raw * factor[:, None, None]


def draw_vectors(key, part):
    first = jax.random.fold_in(key, 37)
    count = FF // D
    total_rows = 8 + count
    base = 0.5 * jax.random.truncated_normal(first, -2.0, 2.0, (total_rows, D), jnp.float32)
    row_index = jnp.arange(total_rows)
    is_gain = (row_index == 0) | (row_index == 5)
    return jnp.where(is_gain[:, None], 1.0 + 0.5 * base, 0.5 * base)


def strengthened(values, stream_key, source, target, shards_of, factor):
    owner, partner = [(jnp.arange(values.shape[position]) // (values.shape[position] // shards_of)).reshape([-1 if axis == position else 1 for axis in range(values.ndim)]) for position in (source, target)]
    chosen = jax.random.permutation(stream_key, shards_of)[partner]
    strong = (owner == chosen) | (owner == (partner + shards_of // 2) % shards_of)
    return jnp.where(strong, factor * values, values)


def block_scale(stream_key, extent, split, least, largest):
    level = 1.0
    for axis_at, blocks in split:
        heights = jax.random.uniform(jax.random.fold_in(jax.random.fold_in(stream_key, 6), axis_at), (blocks,), jnp.float32, least / len(split), largest / len(split))
        level = level * jnp.repeat(jnp.exp(heights), extent[axis_at] // blocks).reshape((-1,) + (1,) * (len(extent) - 1 - axis_at))
    return level


def normal_values(rng, dims, spread, most, pieces=(), kind=jnp.bfloat16):
    array = spread * jax.random.normal(rng, dims, jnp.float32)
    if pieces:
        array = array * block_scale(rng, dims, pieces, -0.22, 0.18)
    return jnp.clip(array, -most, most).astype(kind)


def noise_with(rng, shape, deviation, reach, pieces, heavy, held_as=jnp.bfloat16):
    drawn = deviation * jax.random.normal(rng, shape, jnp.float32)
    if pieces:
        drawn = drawn * block_scale(rng, shape, pieces, -0.22, 0.18)
    return jnp.clip(strengthened(drawn, jax.random.fold_in(rng, 3), *heavy), -reach, reach).astype(held_as)


def setup_inputs(seed: int = 0) -> dict:
    key_of = jax.random.split(jax.random.key(seed), 8)
    block_input_tokens = draw_block_input_tokens(jax.random.fold_in(key_of[7], 71), 0)
    weights = draw_weights(jax.random.fold_in(key_of[7], 71), 0)
    vectors = draw_vectors(jax.random.fold_in(key_of[7], 71), 0)
    momentum = normal_values(key_of[3], (NBLK, D, D), (0.3 * TOKENS ** 0.5), 128.0, ((1, 16), (2, 2)), jnp.float32)
    adam_first = normal_values(key_of[4], (NVEC, D), (0.1 * TOKENS ** 0.5), 48.0, (), jnp.float32)
    adam_second = jnp.clip(jnp.exp(jax.random.uniform(key_of[5], (NVEC, D), jnp.float32, math.log(63.04), math.log(630.4))), 63.04, 630.4)
    output_gradient = noise_with(key_of[6], (TOKENS, D), 1.0, 6.0, ((0, 32),), (0, 1, 32, 2.75), jnp.float32)
    return {"block_input_tokens": block_input_tokens, "weights": weights, "vectors": vectors, "momentum": momentum, "adam_first": adam_first, "adam_second": adam_second, "output_gradient": output_gradient}


eps_norm = 1e-06
momentum_rate = 0.95
muon_rate = 0.1
muon_decay = 0.1
ns_first = 3.4445
ns_second = -4.775
ns_third = 2.0315
adam_rate = 0.1
beta_first = 0.9
beta_second = 0.95
bias_first = 0.19
bias_second = 0.0975
adam_eps = 1e-08
root_half = 0.7071067811865476
inv_root_pi = 0.3989422804014327

def layer_normalize(values, gain_row, shift_row):
    centre = values - lax.optimization_barrier(jnp.mean(values, axis=-1, keepdims=True))
    inverse_std = lax.rsqrt(lax.optimization_barrier(jnp.mean(centre * centre, axis=-1, keepdims=True)) + eps_norm)
    normed = centre * inverse_std
    return (normed * gain_row + shift_row, normed, inverse_std)

def norm_backward_pass(upstream_gradient, gain_row, normed, inverse_std):
    scaled = upstream_gradient * gain_row
    return inverse_std * (scaled - lax.optimization_barrier(jnp.mean(scaled, axis=-1, keepdims=True)) - normed * lax.optimization_barrier(jnp.mean(scaled * normed, axis=-1, keepdims=True)))

def gelu_value(preact):
    return 0.5 * preact * (1.0 + lax.erf(preact * root_half))

def gelu_slope(preact):
    return 0.5 * (1.0 + lax.erf(preact * root_half)) + preact * jnp.exp(-0.5 * preact * preact) * inv_root_pi

def newton_schulz(slab):
    current = slab / (jnp.sqrt(jnp.sum(slab * slab)) + 1e-07)
    for turn_index in range(NS_STEPS):
        gram = jnp.dot(current.T, current, preferred_element_type=jnp.float32, precision=lax.Precision.HIGHEST)
        square = jnp.dot(gram, gram, preferred_element_type=jnp.float32, precision=lax.Precision.HIGHEST)
        poly = ns_second * gram + ns_third * square
        current = ns_first * current + jnp.dot(current, poly, preferred_element_type=jnp.float32, precision=lax.Precision.HIGHEST)
    return current

def reference(block_input_tokens, weights, vectors, momentum, adam_first, adam_second, output_gradient):
    count = FF // D
    blocks = 4 + 2 * count
    group = math.gcd(IMAGES, 16)
    scale = HDIM ** (-0.5)
    cast_w = weights.astype(jnp.bfloat16)
    w_first = cast_w[4:4 + count].astype(jnp.float32)
    w_second = cast_w[4 + count:].astype(jnp.float32)
    bias_hidden = vectors[7:7 + count]

    def heads_view(values):
        return values.reshape(group, SEQ, HEADS, HDIM).astype(jnp.float32)

    def one_group(carry, pair):
        grad_w, grad_v = carry
        input_tokens, upstream_gradient = pair
        n_rows = input_tokens.shape[0]
        first_normed_tokens, first_centred_scaled, first_inverse_deviation = layer_normalize(input_tokens, vectors[0], vectors[1])
        act1 = first_normed_tokens.astype(jnp.bfloat16)
        query = (jnp.dot(act1, cast_w[0], preferred_element_type=jnp.float32) + vectors[2]).astype(jnp.bfloat16)
        keys = jnp.dot(act1, cast_w[1], preferred_element_type=jnp.float32).astype(jnp.bfloat16)
        value = (jnp.dot(act1, cast_w[2], preferred_element_type=jnp.float32) + vectors[3]).astype(jnp.bfloat16)
        query_h = heads_view(query)
        key_h = heads_view(keys)
        value_h = heads_view(value)
        score = jnp.einsum('gqhe,gkhe->ghqk', query_h, key_h) * scale
        peak = lax.optimization_barrier(jnp.max(score, axis=-1, keepdims=True))
        expo = jnp.exp(score - peak)
        total = lax.optimization_barrier(jnp.sum(expo, axis=-1, keepdims=True))
        log_total = peak + jnp.log(total)
        prob_b = (expo / total).astype(jnp.bfloat16)
        mixed = jnp.einsum('ghqk,gkhe->gqhe', prob_b.astype(jnp.float32), value_h).reshape(n_rows, D).astype(jnp.bfloat16)
        residual_stream = input_tokens + (jnp.dot(mixed, cast_w[3].T, preferred_element_type=jnp.float32) + vectors[4])
        second_normed_tokens, second_centred_scaled, second_inverse_deviation = layer_normalize(residual_stream, vectors[5], vectors[6])
        act2 = second_normed_tokens.astype(jnp.bfloat16)
        preact = jnp.einsum('nd,kdj->nkj', act2.astype(jnp.float32), w_first) + bias_hidden[None]
        hidden_b = gelu_value(preact).astype(jnp.bfloat16)
        output = residual_stream + (jnp.einsum('nkj,kej->ne', hidden_b.astype(jnp.float32), w_second) + vectors[7 + count])
        up_b = upstream_gradient.astype(jnp.bfloat16)
        d_hidden = jnp.einsum('ne,kej->nkj', up_b.astype(jnp.float32), w_second)
        preactivation_gradient = d_hidden * gelu_slope(preact)
        d_pre_b = preactivation_gradient.astype(jnp.bfloat16)
        g_first = jnp.einsum('nd,nkj->kdj', act2.astype(jnp.float32), d_pre_b.astype(jnp.float32))
        g_second = jnp.einsum('ne,nkj->kej', up_b.astype(jnp.float32), hidden_b.astype(jnp.float32))
        second_activation_gradient = jnp.einsum('nkj,kdj->nd', d_pre_b.astype(jnp.float32), w_first)
        residual_gradient = upstream_gradient + norm_backward_pass(second_activation_gradient, vectors[5], second_centred_scaled, second_inverse_deviation)
        d_resid_b = residual_gradient.astype(jnp.bfloat16)
        g_out = jnp.dot(d_resid_b.T, mixed, preferred_element_type=jnp.float32)
        d_mixed_b = jnp.dot(d_resid_b, cast_w[3], preferred_element_type=jnp.float32).astype(jnp.bfloat16)
        d_mixed_h = heads_view(d_mixed_b)
        score_again = jnp.einsum('gqhe,gkhe->ghqk', query_h, key_h) * scale
        prob = jnp.exp(score_again - log_total)
        prob_again = prob.astype(jnp.bfloat16)
        value_gradient = jnp.einsum('ghqk,gqhe->gkhe', prob_again.astype(jnp.float32), d_mixed_h).reshape(n_rows, D)
        d_prob = jnp.einsum('gqhe,gkhe->ghqk', d_mixed_h, value_h)
        delta = lax.optimization_barrier(jnp.sum(prob * d_prob, axis=-1, keepdims=True))
        d_score_b = (prob * (d_prob - delta) * scale).astype(jnp.bfloat16).astype(jnp.float32)
        query_gradient = jnp.einsum('ghqk,gkhe->gqhe', d_score_b, key_h).reshape(n_rows, D)
        d_key = jnp.einsum('ghqk,gqhe->gkhe', d_score_b, query_h).reshape(n_rows, D)
        dq_b = query_gradient.astype(jnp.bfloat16)
        dk_b = d_key.astype(jnp.bfloat16)
        dv_b = value_gradient.astype(jnp.bfloat16)
        g_query = jnp.dot(act1.T, dq_b, preferred_element_type=jnp.float32)
        g_key = jnp.dot(act1.T, dk_b, preferred_element_type=jnp.float32)
        g_value = jnp.dot(act1.T, dv_b, preferred_element_type=jnp.float32)
        first_activation_gradient = jnp.dot(dq_b, cast_w[0].T, preferred_element_type=jnp.float32) + jnp.dot(dk_b, cast_w[1].T, preferred_element_type=jnp.float32) + jnp.dot(dv_b, cast_w[2].T, preferred_element_type=jnp.float32)
        input_gradient = residual_gradient + norm_backward_pass(first_activation_gradient, vectors[0], first_centred_scaled, first_inverse_deviation)
        block_grads = jnp.concatenate([jnp.stack([g_query, g_key, g_value, g_out]), g_first, g_second])
        vector_gradients = jnp.concatenate([jnp.stack([lax.optimization_barrier(jnp.sum(first_activation_gradient * first_centred_scaled, axis=0)), lax.optimization_barrier(jnp.sum(first_activation_gradient, axis=0)), lax.optimization_barrier(jnp.sum(query_gradient, axis=0)), lax.optimization_barrier(jnp.sum(value_gradient, axis=0)), lax.optimization_barrier(jnp.sum(residual_gradient, axis=0)), lax.optimization_barrier(jnp.sum(second_activation_gradient * second_centred_scaled, axis=0)), lax.optimization_barrier(jnp.sum(second_activation_gradient, axis=0))]), lax.optimization_barrier(jnp.sum(preactivation_gradient, axis=0)), lax.optimization_barrier(jnp.sum(upstream_gradient, axis=0))[None]])
        return ((grad_w + block_grads, grad_v + vector_gradients), (output, input_gradient))
    inputs_all = block_input_tokens.reshape(IMAGES // group, group * SEQ, D)
    upstream_all = output_gradient.reshape(IMAGES // group, group * SEQ, D)
    start_carry = (jnp.zeros((blocks, D, D), jnp.float32), jnp.zeros((8 + count, D), jnp.float32))
    (weight_grad, vector_grad), (outputs, d_inputs) = lax.scan(one_group, start_carry, (inputs_all, upstream_all))
    new_momentum = momentum_rate * momentum + weight_grad
    halves = N_TENSOR
    slab_w = D // halves
    stacked = new_momentum.reshape(blocks, D, halves, slab_w).transpose(0, 2, 1, 3).reshape(blocks * halves, D, slab_w)
    ortho = lax.map(newton_schulz, stacked)
    ortho = ortho.reshape(blocks, halves, D, slab_w).transpose(0, 2, 1, 3).reshape(blocks, D, D)
    new_weights = weights * (1.0 - muon_rate * muon_decay) - muon_rate * 0.2 * math.sqrt(D) * ortho
    new_adam_first = beta_first * adam_first + (1.0 - beta_first) * vector_grad
    new_adam_second = beta_second * adam_second + (1.0 - beta_second) * vector_grad * vector_grad
    new_vectors = vectors - adam_rate * (new_adam_first / bias_first) / (jnp.sqrt(new_adam_second / bias_second) + adam_eps)
    return (outputs.reshape(TOKENS, D), d_inputs.reshape(TOKENS, D), weight_grad, new_weights, new_momentum, vector_grad, new_vectors, new_adam_first, new_adam_second)
```

```python
import functools
import math

import jax
import jax.numpy as jnp
from jax import lax
from jax.experimental import pallas as pl
from jax.experimental.pallas import tpu as pltpu
from jax.sharding import PartitionSpec as P

HDIM = 64
SEQ = 197
NS_STEPS = 5


eps_norm = 1e-06
momentum_rate = 0.95
muon_rate = 0.1
muon_decay = 0.1
ns_first = 3.4445
ns_second = -4.775
ns_third = 2.0315
adam_rate = 0.1
beta_first = 0.9
beta_second = 0.95
bias_first = 0.19
bias_second = 0.0975
adam_eps = 1e-08
root_half = 0.7071067811865476
inv_root_pi = 0.3989422804014327

f32 = jnp.float32
bf16 = jnp.bfloat16


def layer_normalize(values, gain_row, shift_row):
    centre = values - jnp.mean(values, axis=-1, keepdims=True)
    inverse_std = lax.rsqrt(jnp.mean(centre * centre, axis=-1, keepdims=True) + eps_norm)
    normed = centre * inverse_std
    return (normed * gain_row + shift_row, normed, inverse_std)


def norm_backward_pass(upstream_gradient, gain_row, normed, inverse_std):
    scaled = upstream_gradient * gain_row
    return inverse_std * (
        scaled
        - jnp.mean(scaled, axis=-1, keepdims=True)
        - normed * jnp.mean(scaled * normed, axis=-1, keepdims=True)
    )


def gelu_value(preact):
    return 0.5 * preact * (1.0 + lax.erf(preact * root_half))


def gelu_slope(preact):
    return (
        0.5 * (1.0 + lax.erf(preact * root_half))
        + preact * jnp.exp(-0.5 * preact * preact) * inv_root_pi
    )


def newton_schulz(slab):
    high = lax.Precision.HIGH
    current = slab / (jnp.sqrt(jnp.sum(slab * slab)) + 1e-07)
    for _ in range(NS_STEPS):
        gram = jnp.dot(current.T, current, preferred_element_type=f32, precision=high)
        square = jnp.dot(gram, gram, preferred_element_type=f32, precision=high)
        poly = ns_second * gram + ns_third * square
        current = ns_first * current + jnp.dot(
            current, poly, preferred_element_type=f32, precision=high
        )
    return current


def exchange(array, bit, owners):
    return lax.ppermute(array, "dp", [(i, i ^ bit) for i in range(owners)])


def swap_cores(array):
    return lax.ppermute(array, "tensor", [(0, 1), (1, 0)])


def gather_stage(array, level, levels):
    other = exchange(array, 1 << (levels - 1 - level), 1 << levels)
    return jnp.concatenate([array, other], axis=1 + level)


def scatter_stage(array, level, levels):
    axis = 1 + level
    mine = lax.slice_in_dim(array, 0, 1, axis=axis)
    theirs = lax.slice_in_dim(array, 1, 2, axis=axis)
    came = exchange(theirs, 1 << (levels - 1 - level), 1 << levels)
    return mine.astype(f32) + came.astype(f32)


def gather_chunk(rows, levels):
    blocks, own_rows, width = rows.shape
    array = rows.reshape((blocks,) + (1,) * levels + (own_rows, width))
    for level in range(levels - 2):
        array = gather_stage(array, level, levels)
    first, second = array[: blocks // 2], array[blocks // 2 :]
    first = gather_stage(gather_stage(first, levels - 2, levels), levels - 1, levels)
    second = gather_stage(gather_stage(second, levels - 1, levels), levels - 2, levels)
    return tuple(
        a.reshape(blocks // 2, own_rows << levels, width) for a in (first, second)
    )


def scatter_chunk(first, second, levels):
    blocks, rows, width = first.shape
    shape = (blocks,) + (2,) * levels + (rows >> levels, width)
    first, second = first.reshape(shape), second.reshape(shape)
    first = scatter_stage(first, levels - 1, levels).astype(bf16)
    second = scatter_stage(second, levels - 2, levels).astype(bf16)
    first = scatter_stage(first, levels - 2, levels).astype(bf16)
    second = scatter_stage(second, levels - 1, levels).astype(bf16)
    array = jnp.concatenate([first, second])
    for level in range(levels - 3, -1, -1):
        array = scatter_stage(array, level, levels)
        if level:
            array = array.astype(bf16)
    return array.reshape(2 * blocks, rows >> levels, width)


NN, NT, TN = ((1,), (0,)), ((1,), (1,)), ((0,), (0,))


def dot(left, right, contract=NN):
    return lax.dot_general(left, right, (contract, ((), ())), preferred_element_type=f32)


def params():
    return pltpu.CompilerParams(vmem_limit_bytes=48 * 1024 * 1024)


def column_sum(array):
    return jnp.sum(array, axis=0, keepdims=True)


def softmax_rows(query, key):
    score = dot(query, key, NT) * (HDIM ** (-0.5))
    expo = jnp.exp(score - jnp.max(score, axis=-1, keepdims=True))
    return expo / jnp.sum(expo, axis=-1, keepdims=True)


def attention_forward(
    tokens, vec, core_vec, own_qk, other_qk, own_vo, other_vo,
    act1_out, query_out, key_out, value_out, mixed_out, resid_out, act2_out,
):
    model = tokens.shape[1]
    width = own_qk.shape[2]
    act1 = layer_normalize(tokens[...], vec[0:1], vec[1:2])[0].astype(bf16)
    act1_out[...] = act1
    for k, (qk, vo) in enumerate(((own_qk, own_vo), (other_qk, other_vo))):
        cols = slice(k * width, (k + 1) * width)
        query_out[:, cols] = (dot(act1, qk[0]) + core_vec[2:3, cols]).astype(bf16)
        key_out[:, cols] = dot(act1, qk[1]).astype(bf16)
        value_out[:, cols] = (dot(act1, vo[0]) + core_vec[3:4, cols]).astype(bf16)
    for pair in range(model // (2 * HDIM)):
        lanes = slice(2 * pair * HDIM, 2 * (pair + 1) * HDIM)
        query, key, value = query_out[:, lanes], key_out[:, lanes], value_out[:, lanes]
        parts = []
        for k in range(2):
            head = slice(k * HDIM, (k + 1) * HDIM)
            prob = softmax_rows(query[:, head], key[:, head]).astype(bf16)
            parts.append(dot(prob, value[:, head]))
        mixed_out[:, lanes] = jnp.concatenate(parts, axis=1).astype(bf16)
    resid = (
        tokens[...]
        + (dot(mixed_out[:, :width], own_vo[1], NT) + dot(mixed_out[:, width:], other_vo[1], NT))
        + vec[4:5]
    )
    resid_out[...] = resid
    act2_out[...] = layer_normalize(resid, vec[5:6], vec[6:7])[0].astype(bf16)


def feed_forward(
    act2, up, first, second, bias, mlp_in, d_act2_in,
    g_first, g_second, d_bias, mlp, d_act2,
):
    @pl.when(pl.program_id(0) == 0)
    def _():
        mlp[...] = mlp_in[...]
        d_act2[...] = d_act2_in[...]

    pre = dot(act2[...], first[0]) + bias[0]
    both = 1.0 + lax.erf(pre * root_half)
    hidden = (0.5 * pre * both).astype(bf16)
    slope = 0.5 * both + pre * jnp.exp(-0.5 * pre * pre) * inv_root_pi
    mlp[...] += dot(hidden, second[0], NT)
    g_second[0] = dot(up[...], hidden, TN).astype(bf16)
    d_pre = dot(up[...], second[0]) * slope
    d_bias[0] = column_sum(d_pre)
    d_pre_b = d_pre.astype(bf16)
    g_first[0] = dot(act2[...], d_pre_b, TN).astype(bf16)
    d_act2[...] += dot(d_pre_b, first[0], NT)


def attention_backward(
    d_act2_in, resid, upstream, vec, query_in, key_in, value_in, mixed, own_vo, other_vo,
    d_resid_out, dq_out, dk_out, dv_out, g_out, sums, core_sums,
):
    model = resid.shape[1]
    width = own_vo.shape[2]
    d_act2 = d_act2_in[...]
    _, xhat2, inv2 = layer_normalize(resid[...], vec[5:6], vec[6:7])
    d_resid = upstream[...] + norm_backward_pass(d_act2, vec[5:6], xhat2, inv2)
    d_resid_out[...] = d_resid
    sums[0:1] = column_sum(d_resid)
    sums[1:2] = column_sum(d_act2 * xhat2)
    sums[2:3] = column_sum(d_act2)
    sums[3:4] = column_sum(upstream[...])
    sums[4:8] = jnp.zeros((4, model), f32)
    d_resid_b = d_resid.astype(bf16)
    for k, vo in enumerate((own_vo, other_vo)):
        cols = slice(k * width, (k + 1) * width)
        g_out[k] = dot(d_resid_b, mixed[:, cols], TN).astype(bf16)
        dv_out[:, cols] = dot(d_resid_b, vo[1]).astype(bf16)
    for pair in range(model // (2 * HDIM)):
        lanes = slice(2 * pair * HDIM, 2 * (pair + 1) * HDIM)
        query, key, value, d_mixed = query_in[:, lanes], key_in[:, lanes], value_in[:, lanes], dv_out[:, lanes]
        d_query, d_key, d_value = [], [], []
        for k in range(2):
            head = slice(k * HDIM, (k + 1) * HDIM)
            q, ky, v, dm = query[:, head], key[:, head], value[:, head], d_mixed[:, head]
            prob = softmax_rows(q, ky)
            d_prob = dot(dm, v, NT)
            delta = jnp.sum(prob * d_prob, axis=-1, keepdims=True)
            d_score = (prob * (d_prob - delta) * (HDIM ** (-0.5))).astype(bf16)
            d_value.append(dot(prob.astype(bf16), dm, TN))
            d_query.append(dot(d_score, ky))
            d_key.append(dot(d_score, q, TN))
        d_query, d_key, d_value = [jnp.concatenate(d, axis=1) for d in (d_query, d_key, d_value)]
        core_sums[0:1, lanes] = column_sum(d_query)
        core_sums[1:2, lanes] = column_sum(d_value)
        dq_out[:, lanes] = d_query.astype(bf16)
        dk_out[:, lanes] = d_key.astype(bf16)
        dv_out[:, lanes] = d_value.astype(bf16)
    core_sums[2:8] = jnp.zeros((6, model), f32)


def attention_weight_grads(act1, dq, dk, dv, g_qk, g_v):
    for k in range(2):
        cols = slice(k * g_v.shape[2], (k + 1) * g_v.shape[2])
        g_qk[k, 0] = dot(act1[...], dq[:, cols], TN).astype(bf16)
        g_qk[k, 1] = dot(act1[...], dk[:, cols], TN).astype(bf16)
        g_v[k] = dot(act1[...], dv[:, cols], TN).astype(bf16)


def input_backward(tokens, vec, d_resid, dq, dk, dv, own_qk, other_qk, own_vo, other_vo, grad, sums):
    model = tokens.shape[1]
    width = own_qk.shape[2]
    d_act1 = jnp.zeros(tokens.shape, f32)
    for k, (qk, vo) in enumerate(((own_qk, own_vo), (other_qk, other_vo))):
        cols = slice(k * width, (k + 1) * width)
        d_act1 += dot(dq[:, cols], qk[0], NT)
        d_act1 += dot(dk[:, cols], qk[1], NT)
        d_act1 += dot(dv[:, cols], vo[0], NT)
    _, xhat1, inv1 = layer_normalize(tokens[...], vec[0:1], vec[1:2])
    grad[...] = d_resid[...] + norm_backward_pass(d_act1, vec[0:1], xhat1, inv1)
    sums[0:1] = column_sum(d_act1 * xhat1)
    sums[1:2] = column_sum(d_act1)
    sums[2:8] = jnp.zeros((6, model), f32)


def call(kernel, outs, *args):
    return pl.pallas_call(
        kernel,
        out_shape=[jax.ShapeDtypeStruct(s, d) for s, d in outs],
        compiler_params=params(),
    )(*args)


def shards(
    block_input_tokens, weights, vectors, momentum, adam_first, adam_second, output_gradient
):
    owners = lax.axis_size("dp")
    devices = owners * lax.axis_size("tensor")
    levels = owners.bit_length() - 1
    blocks, own_rows, width = weights.shape
    seq, model = block_input_tokens.shape
    count = (blocks - 4) // 2
    half = count // 2
    here = lax.axis_index("dp")
    core = lax.axis_index("tensor")

    feature = jnp.arange(model)
    source = ((feature // own_rows) ^ here) * own_rows + feature % own_rows
    reorder = (feature[:, None] == source[None, :]).astype(f32)

    def relative(array):
        return jnp.dot(array, reorder, precision=lax.Precision.HIGHEST)

    def halves(row):
        return jnp.where(core == 0, row, jnp.concatenate([row[..., width:], row[..., :width]], -1))

    cast = weights.astype(bf16)
    own_qk, own_vo = gather_chunk(cast[:4], levels)
    other_qk, other_vo = swap_cores(own_qk), swap_cores(own_vo)
    own_ff, other_ff = [], []
    for j in range(2):
        rows = jnp.concatenate([cast[4 + j * half :][:half], cast[4 + count + j * half :][:half]])
        own_ff.append(gather_chunk(rows, levels))
        other_ff.append(tuple(swap_cores(a) for a in own_ff[j]))

    moved = relative(jnp.concatenate([block_input_tokens, output_gradient, vectors]))
    tokens, upstream, vec = moved[:seq], moved[seq : 2 * seq], moved[2 * seq :]
    core_vec = halves(vectors)
    up_b = upstream.astype(bf16)

    wide, wide_b = ((seq, model), f32), ((seq, model), bf16)
    act1, query, key, value, mixed, resid, act2 = call(
        attention_forward,
        [wide_b] * 5 + [wide, wide_b],
        tokens, vec, core_vec, own_qk, other_qk, own_vo, other_vo,
    )

    mlp = resid + vec[7 + count]
    d_act2 = jnp.zeros((seq, model), f32)

    def feed_forward_call(weights_pair, bias, mlp, d_act2):
        whole = pl.BlockSpec((seq, model), lambda k: (0, 0))
        block = pl.BlockSpec((1, model, width), lambda k: (k, 0, 0))
        row = pl.BlockSpec((1, 1, width), lambda k: (k, 0, 0))
        grads = jax.ShapeDtypeStruct((half, model, width), bf16)
        total = jax.ShapeDtypeStruct((seq, model), f32)
        return pl.pallas_call(
            feed_forward,
            grid=(half,),
            in_specs=[whole, whole, block, block, row, whole, whole],
            out_specs=[block, block, row, whole, whole],
            out_shape=[grads, grads, jax.ShapeDtypeStruct((half, 1, width), f32), total, total],
            compiler_params=params(),
        )(act2, up_b, *weights_pair, bias, mlp, d_act2)

    bias_hidden = core_vec[7 : 7 + count].reshape(count, 1, 2, width)
    d_bias, ff_grads = [], []
    for j in range(2):
        parts = []
        for k, pair in enumerate((own_ff[j], other_ff[j])):
            bias = bias_hidden[j * half : (j + 1) * half, :, k]
            g_first, g_second, d_b, mlp, d_act2 = feed_forward_call(pair, bias, mlp, d_act2)
            parts.append((g_first, g_second))
            d_bias.append(d_b)
        came = [swap_cores(g) for g in parts[1]]
        ff_grads.append(
            scatter_chunk(
                *[(g.astype(f32) + c.astype(f32)).astype(bf16) for g, c in zip(parts[0], came)], levels
            )
        )
    output = relative(mlp)

    small = ((8, model), f32)
    d_resid, dq, dk, dv, g_out, sums, core_sums = call(
        attention_backward,
        [wide, wide_b, wide_b, wide_b, ((2, model, width), bf16), small, small],
        d_act2, resid, upstream, vec, query, key, value, mixed, own_vo, other_vo,
    )
    g_qk, g_v = call(
        attention_weight_grads,
        [((2, 2, model, width), bf16), ((2, model, width), bf16)],
        act1, dq, dk, dv,
    )
    g_vo = jnp.stack([g_v, g_out], axis=1)
    g_attn = scatter_chunk(
        *[
            (g[0].astype(f32) + swap_cores(g[1]).astype(f32)).astype(bf16)
            for g in (g_qk, g_vo)
        ],
        levels,
    )
    grad_rel, first_sums = call(
        input_backward,
        [wide, small],
        tokens, vec, d_resid, dq, dk, dv, own_qk, other_qk, own_vo, other_vo,
    )
    input_gradient = relative(grad_rel)

    row_sums = relative(jnp.concatenate([first_sums[:2], sums[:4]]))
    hidden_sums = jnp.concatenate(
        [
            jnp.concatenate([d_bias[2 * j][:, 0], d_bias[2 * j + 1][:, 0]], axis=-1)
            for j in range(2)
        ]
    )
    half_sums = halves(jnp.concatenate([core_sums[:2], hidden_sums]))
    vec_part = jnp.concatenate(
        [row_sums[:2], half_sums[:2], row_sums[2:5], half_sums[2:], row_sums[5:]]
    )
    everywhere = ("dp", "tensor")
    shares = lax.all_to_all(
        vec_part.reshape(devices, -1), everywhere, split_axis=0, concat_axis=0, tiled=True
    )
    summed = jnp.broadcast_to(jnp.sum(shares, axis=0), shares.shape)
    vector_grad = lax.all_to_all(
        summed, everywhere, split_axis=0, concat_axis=0, tiled=True
    ).reshape(vec_part.shape)

    grad_rows = jnp.concatenate(
        [g_attn] + [g[:half] for g in ff_grads] + [g[half:] for g in ff_grads]
    )
    new_momentum = momentum_rate * momentum + grad_rows
    copies = -(-owners // blocks)
    outgoing = jnp.tile(new_momentum.astype(bf16), (copies, 1, 1))[:owners]
    whole_slab = lax.all_to_all(
        outgoing, "dp", split_axis=0, concat_axis=0, tiled=True
    ).reshape(model, width).astype(f32)
    ortho = newton_schulz(whole_slab)
    returned = lax.all_to_all(
        ortho.reshape(owners, own_rows, width).astype(bf16),
        "dp",
        split_axis=0,
        concat_axis=0,
        tiled=True,
    ).astype(f32)[:blocks]
    new_weights = (
        weights * (1.0 - muon_rate * muon_decay) - muon_rate * 0.2 * math.sqrt(model) * returned
    )
    new_adam_first = beta_first * adam_first + (1.0 - beta_first) * vector_grad
    new_adam_second = beta_second * adam_second + (1.0 - beta_second) * vector_grad * vector_grad
    new_vectors = vectors - adam_rate * (new_adam_first / bias_first) / (
        jnp.sqrt(new_adam_second / bias_second) + adam_eps
    )
    return (
        output,
        input_gradient,
        grad_rows,
        new_weights,
        new_momentum,
        vector_grad,
        new_vectors,
        new_adam_first,
        new_adam_second,
    )


def solution(mesh):
    return jax.shard_map(
        shards,
        mesh=mesh,
        in_specs=(
            P(("dp", "tensor"), None),
            P(None, "dp", "tensor"),
            P(),
            P(None, "dp", "tensor"),
            P(),
            P(),
            P(("dp", "tensor"), None),
        ),
        out_specs=(
            P(("dp", "tensor"), None),
            P(("dp", "tensor"), None),
            P(None, "dp", "tensor"),
            P(None, "dp", "tensor"),
            P(None, "dp", "tensor"),
            P(),
            P(),
            P(),
            P(),
        ),
        check_vma=False,
    )
```

```python
import math

import jax
import jax.numpy as jnp
from jax import lax
from jax.experimental import pallas as pl
from jax.experimental.pallas import tpu as pltpu
from jax.sharding import PartitionSpec as P

HDIM = 64
SEQ = 197
NS_STEPS = 5


eps_norm = 1e-06
momentum_rate = 0.95
muon_rate = 0.1
muon_decay = 0.1
ns_first = 3.4445
ns_second = -4.775
ns_third = 2.0315
adam_rate = 0.1
beta_first = 0.9
beta_second = 0.95
bias_first = 0.19
bias_second = 0.0975
adam_eps = 1e-08
root_half = 0.7071067811865476
inv_root_pi = 0.3989422804014327

f32 = jnp.float32
bf16 = jnp.bfloat16


def layer_normalize(values, gain_row, shift_row):
    centre = values - jnp.mean(values, axis=-1, keepdims=True)
    inverse_std = lax.rsqrt(jnp.mean(centre * centre, axis=-1, keepdims=True) + eps_norm)
    normed = centre * inverse_std
    return (normed * gain_row + shift_row, normed, inverse_std)


def norm_backward_pass(upstream_gradient, gain_row, normed, inverse_std):
    scaled = upstream_gradient * gain_row
    return inverse_std * (
        scaled
        - jnp.mean(scaled, axis=-1, keepdims=True)
        - normed * jnp.mean(scaled * normed, axis=-1, keepdims=True)
    )


def gelu_value(preact):
    return 0.5 * preact * (1.0 + lax.erf(preact * root_half))


def gelu_slope(preact):
    return (
        0.5 * (1.0 + lax.erf(preact * root_half))
        + preact * jnp.exp(-0.5 * preact * preact) * inv_root_pi
    )


def exchange(array, bit, owners):
    return lax.ppermute(array, "dp", [(i, i ^ bit) for i in range(owners)])


def swap_cores(array):
    return lax.ppermute(array, "tensor", [(0, 1), (1, 0)])


def gather_stage(array, level, levels, during=()):
    other = after(exchange(array, 1 << (levels - 1 - level), 1 << levels), *during)
    return jnp.concatenate([array, other], axis=1 + level)


def scatter_stage(array, level, levels, during=()):
    axis = 1 + level
    mine = lax.slice_in_dim(array, 0, 1, axis=axis)
    theirs = lax.slice_in_dim(array, 1, 2, axis=axis)
    came = after(exchange(theirs, 1 << (levels - 1 - level), 1 << levels), *during)
    return mine.astype(f32) + came.astype(f32)


def after(array, *earlier):
    return lax.optimization_barrier((array,) + earlier)[0] if earlier else array


NN, NT, TN = ((1,), (0,)), ((1,), (1,)), ((0,), (0,))


def dot(left, right, contract=NN):
    return lax.dot_general(left, right, (contract, ((), ())), preferred_element_type=f32)


def params():
    return pltpu.CompilerParams(vmem_limit_bytes=48 * 1024 * 1024)


def column_sum(array):
    return jnp.sum(array, axis=0, keepdims=True)


def softmax_rows(query, key):
    score = dot(query, key, NT) * (HDIM ** (-0.5))
    expo = jnp.exp(score - jnp.max(score, axis=-1, keepdims=True))
    return expo / jnp.sum(expo, axis=-1, keepdims=True)


def attention_forward(
    tokens, vec, core_vec, own_qk, other_qk, own_vo, other_vo,
    act1_out, query_out, key_out, value_out, mixed_out, resid_out, act2_out,
):
    model = tokens.shape[1]
    width = own_qk.shape[2]
    act1 = layer_normalize(tokens[...], vec[0:1], vec[1:2])[0].astype(bf16)
    act1_out[...] = act1
    for k, (qk, vo) in enumerate(((own_qk, own_vo), (other_qk, other_vo))):
        cols = slice(k * width, (k + 1) * width)
        query_out[:, cols] = (dot(act1, qk[0]) + core_vec[2:3, cols]).astype(bf16)
        key_out[:, cols] = dot(act1, qk[1]).astype(bf16)
        value_out[:, cols] = (dot(act1, vo[0]) + core_vec[3:4, cols]).astype(bf16)
    for pair in range(model // (2 * HDIM)):
        lanes = slice(2 * pair * HDIM, 2 * (pair + 1) * HDIM)
        query, key, value = query_out[:, lanes], key_out[:, lanes], value_out[:, lanes]
        parts = []
        for k in range(2):
            head = slice(k * HDIM, (k + 1) * HDIM)
            prob = softmax_rows(query[:, head], key[:, head]).astype(bf16)
            parts.append(dot(prob, value[:, head]))
        mixed_out[:, lanes] = jnp.concatenate(parts, axis=1).astype(bf16)
    resid = (
        tokens[...]
        + (dot(mixed_out[:, :width], own_vo[1], NT) + dot(mixed_out[:, width:], other_vo[1], NT))
        + vec[4:5]
    )
    resid_out[...] = resid
    act2_out[...] = layer_normalize(resid, vec[5:6], vec[6:7])[0].astype(bf16)


def feed_forward(
    act2, up, first, second, bias, mlp_in, d_act2_in,
    g_first, g_second, d_bias, mlp, d_act2,
):
    @pl.when(pl.program_id(0) == 0)
    def _():
        mlp[...] = mlp_in[...]
        d_act2[...] = d_act2_in[...]

    pre = dot(act2[...], first[0]) + bias[0]
    both = 1.0 + lax.erf(pre * root_half)
    hidden = (0.5 * pre * both).astype(bf16)
    slope = 0.5 * both + pre * jnp.exp(-0.5 * pre * pre) * inv_root_pi
    mlp[...] += dot(hidden, second[0], NT)
    g_second[0] = dot(up[...], hidden, TN).astype(bf16)
    d_pre = dot(up[...], second[0]) * slope
    d_bias[0] = column_sum(d_pre)
    d_pre_b = d_pre.astype(bf16)
    g_first[0] = dot(act2[...], d_pre_b, TN).astype(bf16)
    d_act2[...] += dot(d_pre_b, first[0], NT)


def residual_backward(
    d_act2_in, resid, upstream, vec, mixed, own_vo, other_vo, d_resid_out, d_mixed_out, g_out, sums
):
    model = resid.shape[1]
    width = own_vo.shape[2]
    d_act2 = d_act2_in[...]
    _, xhat2, inv2 = layer_normalize(resid[...], vec[5:6], vec[6:7])
    d_resid = upstream[...] + norm_backward_pass(d_act2, vec[5:6], xhat2, inv2)
    d_resid_out[...] = d_resid
    sums[0:1] = column_sum(d_resid)
    sums[1:2] = column_sum(d_act2 * xhat2)
    sums[2:3] = column_sum(d_act2)
    sums[3:4] = column_sum(upstream[...])
    sums[4:8] = jnp.zeros((4, model), f32)
    d_resid_b = d_resid.astype(bf16)
    for k, vo in enumerate((own_vo, other_vo)):
        cols = slice(k * width, (k + 1) * width)
        g_out[k] = dot(d_resid_b, mixed[:, cols], TN).astype(bf16)
        d_mixed_out[:, cols] = dot(d_resid_b, vo[1]).astype(bf16)


def attention_backward(query_in, key_in, value_in, d_mixed_in, dq_out, dk_out, dv_out, core_sums):
    model = query_in.shape[1]
    for pair in range(model // (2 * HDIM)):
        lanes = slice(2 * pair * HDIM, 2 * (pair + 1) * HDIM)
        query, key, value, d_mixed = query_in[:, lanes], key_in[:, lanes], value_in[:, lanes], d_mixed_in[:, lanes]
        d_query, d_key, d_value = [], [], []
        for k in range(2):
            head = slice(k * HDIM, (k + 1) * HDIM)
            q, ky, v, dm = query[:, head], key[:, head], value[:, head], d_mixed[:, head]
            prob = softmax_rows(q, ky)
            d_prob = dot(dm, v, NT)
            delta = jnp.sum(prob * d_prob, axis=-1, keepdims=True)
            d_score = (prob * (d_prob - delta) * (HDIM ** (-0.5))).astype(bf16)
            d_value.append(dot(prob.astype(bf16), dm, TN))
            d_query.append(dot(d_score, ky))
            d_key.append(dot(d_score, q, TN))
        d_query, d_key, d_value = [jnp.concatenate(d, axis=1) for d in (d_query, d_key, d_value)]
        core_sums[0:1, lanes] = column_sum(d_query)
        core_sums[1:2, lanes] = column_sum(d_value)
        dq_out[:, lanes] = d_query.astype(bf16)
        dk_out[:, lanes] = d_key.astype(bf16)
        dv_out[:, lanes] = d_value.astype(bf16)
    core_sums[2:8] = jnp.zeros((6, model), f32)


def attention_weight_grads(act1, dq, dk, dv, g_qk, g_v):
    for k in range(2):
        cols = slice(k * g_v.shape[2], (k + 1) * g_v.shape[2])
        g_qk[k, 0] = dot(act1[...], dq[:, cols], TN).astype(bf16)
        g_qk[k, 1] = dot(act1[...], dk[:, cols], TN).astype(bf16)
        g_v[k] = dot(act1[...], dv[:, cols], TN).astype(bf16)


def input_backward(tokens, vec, d_resid, dq, dk, dv, own_qk, other_qk, own_vo, other_vo, grad, sums):
    model = tokens.shape[1]
    width = own_qk.shape[2]
    d_act1 = jnp.zeros(tokens.shape, f32)
    for k, (qk, vo) in enumerate(((own_qk, own_vo), (other_qk, other_vo))):
        cols = slice(k * width, (k + 1) * width)
        d_act1 += dot(dq[:, cols], qk[0], NT)
        d_act1 += dot(dk[:, cols], qk[1], NT)
        d_act1 += dot(dv[:, cols], vo[0], NT)
    _, xhat1, inv1 = layer_normalize(tokens[...], vec[0:1], vec[1:2])
    grad[...] = d_resid[...] + norm_backward_pass(d_act1, vec[0:1], xhat1, inv1)
    sums[0:1] = column_sum(d_act1 * xhat1)
    sums[1:2] = column_sum(d_act1)
    sums[2:8] = jnp.zeros((6, model), f32)


def halve(array):
    high = array.astype(bf16)
    return high, (array - high.astype(f32)).astype(bf16)


def newton_schulz(slab, out):
    values = slab[...].astype(f32)
    current = values / (jnp.sqrt(jnp.sum(values * values)) + 1e-07)
    width = values.shape[1]
    for _ in range(NS_STEPS):
        high, low = halve(current)
        product = dot(high, jnp.concatenate([high, low], axis=1), TN)
        mixed = product[:, width:]
        gram = product[:, :width] + (mixed + mixed.T)
        gram_high, gram_low = halve(gram)
        product = dot(gram_high, jnp.concatenate([gram_high, gram_low], axis=1))
        mixed = product[:, width:]
        square = product[:, :width] + (mixed + mixed.T)
        poly_high, poly_low = halve(ns_second * gram + ns_third * square)
        product = dot(high, jnp.concatenate([poly_high, poly_low], axis=1))
        current = ns_first * current + (
            product[:, :width] + (product[:, width:] + dot(low, poly_high))
        )
    out[...] = current.astype(bf16)


def call(kernel, outs, *args):
    return pl.pallas_call(
        kernel,
        out_shape=[jax.ShapeDtypeStruct(s, d) for s, d in outs],
        compiler_params=params(),
    )(*args)


def shards(
    block_input_tokens, weights, vectors, momentum, adam_first, adam_second, output_gradient
):
    owners = lax.axis_size("dp")
    levels = owners.bit_length() - 1
    blocks, own_rows, width = weights.shape
    seq, model = block_input_tokens.shape
    count = (blocks - 4) // 2
    half = count // 2
    here = lax.axis_index("dp")
    core = lax.axis_index("tensor")

    feature = jnp.arange(model)
    source = ((feature // own_rows) ^ here) * own_rows + feature % own_rows
    reorder = (feature[:, None] == source[None, :]).astype(f32)

    def relative(array):
        return jnp.dot(array, reorder, precision=lax.Precision.HIGHEST)

    def halves(row):
        return jnp.where(core == 0, row, jnp.concatenate([row[..., width:], row[..., :width]], -1))

    cast = weights.astype(bf16)
    last, before = levels - 1, levels - 2
    z_levels = list(range(levels - 2))

    def stage(array, level, *earlier, during=()):
        return gather_stage(after(array, *earlier), level, levels, during)

    def whole(array):
        return array.reshape(array.shape[0], own_rows << levels, width)

    def chunk(*starts):
        array = jnp.concatenate([cast[i : i + half] for i in starts])
        return array.reshape((2 * half,) + (1,) * levels + (own_rows, width))

    def over_z(array, first_after, then_after):
        array = stage(array, z_levels[0], *first_after)
        first = array
        for level in z_levels[1:]:
            array = stage(array, level, *then_after)
            then_after = ()
        return first, array

    def over_one(array, *earlier):
        return [
            stage(array[half * k : half * (k + 1)], level, *earlier)
            for k, level in ((0, before), (1, last))
        ]

    def over_two(pair, *earlier, during=()):
        return [
            whole(stage(one, level, *earlier, during=during))
            for one, level in zip(pair, (last, before))
        ]

    first_a, z_a = over_z(chunk(0, 2), (), ())
    first_b, z_b = over_z(chunk(4, 4 + count), (first_a,), ())
    one_a = over_one(z_a, first_b)
    first_c, z_c = over_z(chunk(4 + half, 4 + count + half), (first_b,), ())
    own_qk, own_vo = over_two(one_a)
    one_b = over_one(z_b, first_c, *one_a)
    other_qk, other_vo = [swap_cores(a) for a in (own_qk, own_vo)]
    one_c = over_one(z_c, *one_b)

    moved = relative(jnp.concatenate([block_input_tokens, output_gradient, vectors]))
    tokens, upstream, vec = moved[:seq], moved[seq : 2 * seq], moved[2 * seq :]
    core_vec = halves(vectors)
    up_b = upstream.astype(bf16)

    wide, wide_b = ((seq, model), f32), ((seq, model), bf16)
    act1, query, key, value, mixed, resid, act2 = call(
        attention_forward,
        [wide_b] * 5 + [wide, wide_b],
        tokens, vec, core_vec, own_qk, other_qk, own_vo, other_vo,
    )

    two_b = over_two(one_b, z_c, during=(act1,))
    other_b = [swap_cores(after(a, *one_c)) for a in two_b]

    mlp = resid + vec[7 + count]
    d_act2 = jnp.zeros((seq, model), f32)

    def feed_forward_call(weights_pair, bias, mlp, d_act2):
        whole = pl.BlockSpec((seq, model), lambda k: (0, 0))
        block = pl.BlockSpec((1, model, width), lambda k: (k, 0, 0))
        row = pl.BlockSpec((1, 1, width), lambda k: (k, 0, 0))
        grads = jax.ShapeDtypeStruct((half, model, width), bf16)
        total = jax.ShapeDtypeStruct((seq, model), f32)
        return pl.pallas_call(
            feed_forward,
            grid=(half,),
            in_specs=[whole, whole, block, block, row, whole, whole],
            out_specs=[block, block, row, whole, whole],
            out_shape=[grads, grads, jax.ShapeDtypeStruct((half, 1, width), f32), total, total],
            compiler_params=params(),
        )(act2, up_b, *weights_pair, bias, mlp, d_act2)

    bias_hidden = core_vec[7 : 7 + count].reshape(count, 1, 2, width)
    def bias_of(j, k):
        return bias_hidden[j * half : (j + 1) * half, :, k]

    def over_cores(own, other, *during):
        return [
            (g.astype(f32) + after(swap_cores(o), *during).astype(f32)).astype(bf16)
            for g, o in zip(own, other)
        ]

    *grads_0, bias_0, mlp, d_act2 = feed_forward_call(two_b, bias_of(0, 0), mlp, after(d_act2, *one_c))
    other_b = [after(a, d_act2) for a in other_b]
    *grads_1, bias_1, mlp, d_act2 = feed_forward_call(other_b, bias_of(0, 1), mlp, d_act2)
    two_c = over_two(one_c, during=(d_act2,))
    sent_b = over_cores(grads_0, grads_1)
    d_act2 = after(d_act2, *sent_b)
    *grads_0, bias_2, mlp, d_act2 = feed_forward_call(two_c, bias_of(1, 0), mlp, d_act2)
    other_c = [after(swap_cores(a), d_act2) for a in two_c]
    *grads_1, bias_3, mlp, d_act2 = feed_forward_call(other_c, bias_of(1, 1), mlp, d_act2)
    sent_c = over_cores(grads_0, grads_1)
    d_bias = [bias_0, bias_1, bias_2, bias_3]

    def cut(array, level, *earlier, during=()):
        return scatter_stage(after(array.astype(bf16), *earlier), level, levels, during)

    def grown(array):
        return array.reshape((array.shape[0],) + (2,) * levels + (own_rows, width))

    def join(pair):
        return jnp.concatenate([p.astype(bf16) for p in pair])

    sent_b, sent_c = [[grown(a) for a in part] for part in (sent_b, sent_c)]
    one_b = [cut(a, level, during=(d_act2,)) for a, level in zip(sent_b, (last, before))]
    output = relative(mlp)

    small = ((8, model), f32)
    d_resid, d_mixed, g_out, sums = call(
        residual_backward,
        [wide, wide_b, ((2, model, width), bf16), small],
        d_act2, resid, upstream, vec, mixed, own_vo, other_vo,
    )
    dq, dk, dv, core_sums = call(
        attention_backward,
        [wide_b, wide_b, wide_b, small],
        query, key, value, after(d_mixed, *sent_c),
    )
    g_qk, g_v = call(
        attention_weight_grads,
        [((2, 2, model, width), bf16), ((2, model, width), bf16)],
        after(act1, *one_b), dq, dk, dv,
    )
    grad_rel, first_sums = call(
        input_backward,
        [wide, small],
        after(tokens, g_qk), vec, d_resid, dq, dk, dv, own_qk, other_qk, own_vo, other_vo,
    )
    g_vo = jnp.stack([g_v, g_out], axis=1)
    sent_a = over_cores((g_qk[0], g_vo[0]), (g_qk[1], g_vo[1]))
    sent_a = [grown(a) for a in sent_a]
    one_c = [cut(a, level, during=(dq,)) for a, level in zip(sent_c, (last, before))]
    two_b = [cut(a, level, during=(dq,)) for a, level in zip(one_b, (before, last))]
    one_a = [cut(a, level) for a, level in zip(sent_a, (last, before))]
    two_c = [cut(a, level, *sent_a) for a, level in zip(one_c, (before, last))]
    z_b = cut(join(two_b), z_levels[-1], *sent_a)
    two_a = [cut(a, level, *two_b) for a, level in zip(one_a, (before, last))]
    for level in z_levels[-2::-1]:
        z_b = cut(z_b, level, *one_a)
    z_c = cut(join(two_c), z_levels[-1], z_b)
    z_a = cut(join(two_a), z_levels[-1], z_c)
    for level in z_levels[-2::-1]:
        z_c = cut(z_c, level)
    for level in z_levels[-2::-1]:
        z_a = cut(z_a, level, z_c)
    rows_a, rows_b, rows_c = [a.reshape(2 * half, own_rows, width) for a in (z_a, z_b, z_c)]
    input_gradient = relative(grad_rel)

    row_sums = relative(jnp.concatenate([first_sums[:2], sums[:4]]))
    hidden_sums = jnp.concatenate(
        [
            jnp.concatenate([d_bias[2 * j][:, 0], d_bias[2 * j + 1][:, 0]], axis=-1)
            for j in range(2)
        ]
    )
    half_sums = halves(jnp.concatenate([core_sums[:2], hidden_sums]))
    vec_part = jnp.concatenate(
        [row_sums[:2], half_sums[:2], row_sums[2:5], half_sums[2:], row_sums[5:]]
    )

    def add_rounds(values, *bits):
        came = [exchange(values, k, owners) for k in bits]
        values = values + came[0]
        if len(bits) == 3:
            values = values + (came[1] + came[2])
        return values

    vector_grad = vec_part + swap_cores(vec_part)
    for k in range(0, levels - 1, 2):
        vector_grad = add_rounds(vector_grad, 1 << k, 2 << k, 3 << k)
    if levels % 2:
        vector_grad = add_rounds(vector_grad, 1 << (levels - 1))
    grad_rows = jnp.concatenate(
        [rows_a, rows_b[:half], rows_c[:half], rows_b[half:], rows_c[half:]]
    )
    new_momentum = momentum_rate * momentum + grad_rows
    outgoing = new_momentum.astype(bf16)
    outgoing = jnp.concatenate([outgoing] * (owners // blocks) + [outgoing[: owners % blocks]])
    whole_slab = lax.all_to_all(
        outgoing, "dp", split_axis=0, concat_axis=0, tiled=True
    ).reshape(model, width)
    ortho = call(newton_schulz, [((model, width), bf16)], whole_slab)[0]
    returned = lax.all_to_all(
        ortho.reshape(owners, own_rows, width),
        "dp",
        split_axis=0,
        concat_axis=0,
        tiled=True,
    ).astype(f32)[:blocks]
    new_weights = (
        weights * (1.0 - muon_rate * muon_decay) - muon_rate * 0.2 * math.sqrt(model) * returned
    )
    new_adam_first = beta_first * adam_first + (1.0 - beta_first) * vector_grad
    new_adam_second = beta_second * adam_second + (1.0 - beta_second) * vector_grad * vector_grad
    new_vectors = vectors - adam_rate * (new_adam_first / bias_first) / (
        jnp.sqrt(new_adam_second / bias_second) + adam_eps
    )
    return (
        output,
        input_gradient,
        grad_rows,
        new_weights,
        new_momentum,
        vector_grad,
        new_vectors,
        new_adam_first,
        new_adam_second,
    )


def solution(mesh):
    return jax.shard_map(
        shards,
        mesh=mesh,
        in_specs=(
            P(("dp", "tensor"), None),
            P(None, "dp", "tensor"),
            P(),
            P(None, "dp", "tensor"),
            P(),
            P(),
            P(("dp", "tensor"), None),
        ),
        out_specs=(
            P(("dp", "tensor"), None),
            P(("dp", "tensor"), None),
            P(None, "dp", "tensor"),
            P(None, "dp", "tensor"),
            P(None, "dp", "tensor"),
            P(),
            P(),
            P(),
            P(),
        ),
        check_vma=False,
    )
```

```python
import math

import jax
import jax.numpy as jnp
from jax import lax
from jax.experimental import pallas as pl
from jax.experimental.pallas import tpu as pltpu
from jax.sharding import PartitionSpec as P

HDIM = 64
SEQ = 197
NS_STEPS = 5


eps_norm = 1e-06
momentum_rate = 0.95
muon_rate = 0.1
muon_decay = 0.1
ns_first = 3.4445
ns_second = -4.775
ns_third = 2.0315
adam_rate = 0.1
beta_first = 0.9
beta_second = 0.95
bias_first = 0.19
bias_second = 0.0975
adam_eps = 1e-08
root_half = 0.7071067811865476
inv_root_pi = 0.3989422804014327

f32 = jnp.float32
bf16 = jnp.bfloat16


def layer_normalize(values, gain_row, shift_row):
    centre = values - jnp.mean(values, axis=-1, keepdims=True)
    inverse_std = lax.rsqrt(jnp.mean(centre * centre, axis=-1, keepdims=True) + eps_norm)
    normed = centre * inverse_std
    return (normed * gain_row + shift_row, normed, inverse_std)


def norm_backward_pass(upstream_gradient, gain_row, normed, inverse_std):
    scaled = upstream_gradient * gain_row
    return inverse_std * (
        scaled
        - jnp.mean(scaled, axis=-1, keepdims=True)
        - normed * jnp.mean(scaled * normed, axis=-1, keepdims=True)
    )


def gelu_value(preact):
    return 0.5 * preact * (1.0 + lax.erf(preact * root_half))


def gelu_slope(preact):
    return (
        0.5 * (1.0 + lax.erf(preact * root_half))
        + preact * jnp.exp(-0.5 * preact * preact) * inv_root_pi
    )


def exchange(array, bit, owners):
    return lax.ppermute(array, "dp", [(i, i ^ bit) for i in range(owners)])


def swap_cores(array):
    return lax.ppermute(array, "tensor", [(0, 1), (1, 0)])


def gather_stage(array, level, levels, during=()):
    other = after(exchange(array, 1 << (levels - 1 - level), 1 << levels), *during)
    return jnp.concatenate([array, other], axis=1 + level)


def scatter_stage(array, level, levels, during=()):
    axis = 1 + level
    mine = lax.slice_in_dim(array, 0, 1, axis=axis)
    theirs = lax.slice_in_dim(array, 1, 2, axis=axis)
    came = after(exchange(theirs, 1 << (levels - 1 - level), 1 << levels), *during)
    return mine.astype(f32) + came.astype(f32)


def tie(*arrays):
    return lax.optimization_barrier(arrays)


def after(array, *earlier):
    return lax.optimization_barrier((array,) + earlier)[0] if earlier else array


NN, NT, TN = ((1,), (0,)), ((1,), (1,)), ((0,), (0,))


def dot(left, right, contract=NN):
    return lax.dot_general(left, right, (contract, ((), ())), preferred_element_type=f32)


def params():
    return pltpu.CompilerParams(vmem_limit_bytes=48 * 1024 * 1024)


def column_sum(array):
    return jnp.sum(array, axis=0, keepdims=True)


def softmax_rows(query, key):
    score = dot(query, key, NT) * (HDIM ** (-0.5))
    expo = jnp.exp(score - jnp.max(score, axis=-1, keepdims=True))
    return expo / jnp.sum(expo, axis=-1, keepdims=True)


def attention_forward(
    tokens, vec, core_vec, own_qk, other_qk, own_vo, other_vo,
    act1_out, query_out, key_out, value_out, mixed_out, resid_out, act2_out,
):
    model = tokens.shape[1]
    width = own_qk.shape[2]
    act1 = layer_normalize(tokens[...], vec[0:1], vec[1:2])[0].astype(bf16)
    act1_out[...] = act1
    for k, (qk, vo) in enumerate(((own_qk, own_vo), (other_qk, other_vo))):
        cols = slice(k * width, (k + 1) * width)
        query_out[:, cols] = (dot(act1, qk[0]) + core_vec[2:3, cols]).astype(bf16)
        key_out[:, cols] = dot(act1, qk[1]).astype(bf16)
        value_out[:, cols] = (dot(act1, vo[0]) + core_vec[3:4, cols]).astype(bf16)
    for pair in range(model // (2 * HDIM)):
        lanes = slice(2 * pair * HDIM, 2 * (pair + 1) * HDIM)
        query, key, value = query_out[:, lanes], key_out[:, lanes], value_out[:, lanes]
        parts = []
        for k in range(2):
            head = slice(k * HDIM, (k + 1) * HDIM)
            prob = softmax_rows(query[:, head], key[:, head]).astype(bf16)
            parts.append(dot(prob, value[:, head]))
        mixed_out[:, lanes] = jnp.concatenate(parts, axis=1).astype(bf16)
    resid = (
        tokens[...]
        + (dot(mixed_out[:, :width], own_vo[1], NT) + dot(mixed_out[:, width:], other_vo[1], NT))
        + vec[4:5]
    )
    resid_out[...] = resid
    act2_out[...] = layer_normalize(resid, vec[5:6], vec[6:7])[0].astype(bf16)


def feed_forward(
    act2, up, first, second, bias, mlp_in, d_act2_in,
    g_first, g_second, d_bias, mlp, d_act2,
):
    @pl.when(pl.program_id(0) == 0)
    def _():
        mlp[...] = mlp_in[...]
        d_act2[...] = d_act2_in[...]

    pre = dot(act2[...], first[0]) + bias[0]
    both = 1.0 + lax.erf(pre * root_half)
    hidden = (0.5 * pre * both).astype(bf16)
    slope = 0.5 * both + pre * jnp.exp(-0.5 * pre * pre) * inv_root_pi
    mlp[...] += dot(hidden, second[0], NT)
    g_second[0] = dot(up[...], hidden, TN).astype(bf16)
    d_pre = dot(up[...], second[0]) * slope
    d_bias[0] = column_sum(d_pre)
    d_pre_b = d_pre.astype(bf16)
    g_first[0] = dot(act2[...], d_pre_b, TN).astype(bf16)
    d_act2[...] += dot(d_pre_b, first[0], NT)


def residual_backward(
    d_act2_in, resid, upstream, vec, mixed, own_vo, other_vo, d_resid_out, d_mixed_out, g_out, sums
):
    model = resid.shape[1]
    width = own_vo.shape[2]
    d_act2 = d_act2_in[...]
    _, xhat2, inv2 = layer_normalize(resid[...], vec[5:6], vec[6:7])
    d_resid = upstream[...] + norm_backward_pass(d_act2, vec[5:6], xhat2, inv2)
    d_resid_out[...] = d_resid
    sums[0:1] = column_sum(d_resid)
    sums[1:2] = column_sum(d_act2 * xhat2)
    sums[2:3] = column_sum(d_act2)
    sums[3:4] = column_sum(upstream[...])
    sums[4:8] = jnp.zeros((4, model), f32)
    d_resid_b = d_resid.astype(bf16)
    for k, vo in enumerate((own_vo, other_vo)):
        cols = slice(k * width, (k + 1) * width)
        g_out[k] = dot(d_resid_b, mixed[:, cols], TN).astype(bf16)
        d_mixed_out[:, cols] = dot(d_resid_b, vo[1]).astype(bf16)


def attention_backward(query_in, key_in, value_in, d_mixed_in, dq_out, dk_out, dv_out, core_sums):
    model = query_in.shape[1]
    for pair in range(model // (2 * HDIM)):
        lanes = slice(2 * pair * HDIM, 2 * (pair + 1) * HDIM)
        query, key, value, d_mixed = query_in[:, lanes], key_in[:, lanes], value_in[:, lanes], d_mixed_in[:, lanes]
        d_query, d_key, d_value = [], [], []
        for k in range(2):
            head = slice(k * HDIM, (k + 1) * HDIM)
            q, ky, v, dm = query[:, head], key[:, head], value[:, head], d_mixed[:, head]
            prob = softmax_rows(q, ky)
            d_prob = dot(dm, v, NT)
            delta = jnp.sum(prob * d_prob, axis=-1, keepdims=True)
            d_score = (prob * (d_prob - delta) * (HDIM ** (-0.5))).astype(bf16)
            d_value.append(dot(prob.astype(bf16), dm, TN))
            d_query.append(dot(d_score, ky))
            d_key.append(dot(d_score, q, TN))
        d_query, d_key, d_value = [jnp.concatenate(d, axis=1) for d in (d_query, d_key, d_value)]
        core_sums[0:1, lanes] = column_sum(d_query)
        core_sums[1:2, lanes] = column_sum(d_value)
        dq_out[:, lanes] = d_query.astype(bf16)
        dk_out[:, lanes] = d_key.astype(bf16)
        dv_out[:, lanes] = d_value.astype(bf16)
    core_sums[2:8] = jnp.zeros((6, model), f32)


def attention_weight_grads(act1, dq, dk, dv, g_qk, g_v):
    for k in range(2):
        cols = slice(k * g_v.shape[2], (k + 1) * g_v.shape[2])
        g_qk[k, 0] = dot(act1[...], dq[:, cols], TN).astype(bf16)
        g_qk[k, 1] = dot(act1[...], dk[:, cols], TN).astype(bf16)
        g_v[k] = dot(act1[...], dv[:, cols], TN).astype(bf16)


def input_backward(tokens, vec, d_resid, dq, dk, dv, own_qk, other_qk, own_vo, other_vo, grad, sums):
    model = tokens.shape[1]
    width = own_qk.shape[2]
    d_act1 = jnp.zeros(tokens.shape, f32)
    for k, (qk, vo) in enumerate(((own_qk, own_vo), (other_qk, other_vo))):
        cols = slice(k * width, (k + 1) * width)
        d_act1 += dot(dq[:, cols], qk[0], NT)
        d_act1 += dot(dk[:, cols], qk[1], NT)
        d_act1 += dot(dv[:, cols], vo[0], NT)
    _, xhat1, inv1 = layer_normalize(tokens[...], vec[0:1], vec[1:2])
    grad[...] = d_resid[...] + norm_backward_pass(d_act1, vec[0:1], xhat1, inv1)
    sums[0:1] = column_sum(d_act1 * xhat1)
    sums[1:2] = column_sum(d_act1)
    sums[2:8] = jnp.zeros((6, model), f32)


def halve(array):
    high = array.astype(bf16)
    return high, (array - high.astype(f32)).astype(bf16)


def newton_schulz(slab, out):
    values = slab[...].astype(f32)
    current = values / (jnp.sqrt(jnp.sum(values * values)) + 1e-07)
    width = values.shape[1]
    for _ in range(NS_STEPS):
        high, low = halve(current)
        product = dot(high, jnp.concatenate([high, low], axis=1), TN)
        mixed = product[:, width:]
        gram = product[:, :width] + (mixed + mixed.T)
        gram_high, gram_low = halve(gram)
        product = dot(gram_high, jnp.concatenate([gram_high, gram_low], axis=1))
        mixed = product[:, width:]
        square = product[:, :width] + (mixed + mixed.T)
        poly_high, poly_low = halve(ns_second * gram + ns_third * square)
        product = dot(high, jnp.concatenate([poly_high, poly_low], axis=1))
        current = ns_first * current + (
            product[:, :width] + (product[:, width:] + dot(low, poly_high))
        )
    out[...] = current.astype(bf16)


def call(kernel, outs, *args):
    return pl.pallas_call(
        kernel,
        out_shape=[jax.ShapeDtypeStruct(s, d) for s, d in outs],
        compiler_params=params(),
    )(*args)


def shards(
    block_input_tokens, weights, vectors, momentum, adam_first, adam_second, output_gradient
):
    owners = lax.axis_size("dp")
    levels = owners.bit_length() - 1
    blocks, own_rows, width = weights.shape
    seq, model = block_input_tokens.shape
    count = (blocks - 4) // 2
    half = count // 2
    here = lax.axis_index("dp")
    core = lax.axis_index("tensor")

    feature = jnp.arange(model)
    source = ((feature // own_rows) ^ here) * own_rows + feature % own_rows
    reorder = (feature[:, None] == source[None, :]).astype(f32)

    def relative(array):
        return jnp.dot(array, reorder, precision=lax.Precision.HIGHEST)

    def halves(row):
        return jnp.where(core == 0, row, jnp.concatenate([row[..., width:], row[..., :width]], -1))

    cast = weights.astype(bf16)
    last, before = levels - 1, levels - 2
    z_levels = list(range(levels - 2))

    def stage(array, level, *earlier, during=()):
        return gather_stage(after(array, *earlier), level, levels, during)

    def whole(array):
        return array.reshape(array.shape[0], own_rows << levels, width)

    def chunk(*starts):
        array = jnp.concatenate([cast[i : i + half] for i in starts])
        return array.reshape((2 * half,) + (1,) * levels + (own_rows, width))

    def over_z(array, first_after, then_after):
        array = stage(array, z_levels[0], *first_after)
        first = array
        for level in z_levels[1:]:
            array = stage(array, level, *then_after)
            then_after = ()
        return first, array

    def over_one(array, *earlier):
        return [
            stage(array[half * k : half * (k + 1)], level, *earlier)
            for k, level in ((0, before), (1, last))
        ]

    def over_two(pair, *earlier, during=()):
        return [
            whole(stage(one, level, *earlier, during=during))
            for one, level in zip(pair, (last, before))
        ]

    first_a, z_a = over_z(chunk(0, 2), (), ())
    first_b, z_b = over_z(chunk(4, 4 + count), (first_a,), ())
    one_a = over_one(z_a, first_b)
    first_c, z_c = over_z(chunk(4 + half, 4 + count + half), (first_b,), ())
    own_qk, own_vo = over_two(one_a)
    one_b = over_one(z_b, first_c, *one_a)
    other_qk, other_vo = [swap_cores(a) for a in (own_qk, own_vo)]
    one_c = over_one(z_c, *one_b)

    moved = relative(jnp.concatenate([block_input_tokens, output_gradient, vectors]))
    tokens, upstream, vec = moved[:seq], moved[seq : 2 * seq], moved[2 * seq :]
    core_vec = halves(vectors)
    up_b = upstream.astype(bf16)

    wide, wide_b = ((seq, model), f32), ((seq, model), bf16)
    act1, query, key, value, mixed, resid, act2 = call(
        attention_forward,
        [wide_b] * 5 + [wide, wide_b],
        tokens, vec, core_vec, own_qk, other_qk, own_vo, other_vo,
    )

    two_b = over_two(one_b, z_c, during=(act1,))
    other_b = [swap_cores(after(a, *one_c)) for a in two_b]

    mlp = resid + vec[7 + count]
    d_act2 = jnp.zeros((seq, model), f32)

    def feed_forward_call(weights_pair, bias, mlp, d_act2):
        whole = pl.BlockSpec((seq, model), lambda k: (0, 0))
        block = pl.BlockSpec((1, model, width), lambda k: (k, 0, 0))
        row = pl.BlockSpec((1, 1, width), lambda k: (k, 0, 0))
        grads = jax.ShapeDtypeStruct((half, model, width), bf16)
        total = jax.ShapeDtypeStruct((seq, model), f32)
        return pl.pallas_call(
            feed_forward,
            grid=(half,),
            in_specs=[whole, whole, block, block, row, whole, whole],
            out_specs=[block, block, row, whole, whole],
            out_shape=[grads, grads, jax.ShapeDtypeStruct((half, 1, width), f32), total, total],
            compiler_params=params(),
        )(act2, up_b, *weights_pair, bias, mlp, d_act2)

    bias_hidden = core_vec[7 : 7 + count].reshape(count, 1, 2, width)
    def bias_of(j, k):
        return bias_hidden[j * half : (j + 1) * half, :, k]

    def over_cores(own, other, *during):
        return [
            (g.astype(f32) + after(swap_cores(o), *during).astype(f32)).astype(bf16)
            for g, o in zip(own, other)
        ]

    *grads_0, bias_0, mlp, d_act2 = feed_forward_call(two_b, bias_of(0, 0), mlp, after(d_act2, *one_c))
    other_b = [after(a, d_act2) for a in other_b]
    *grads_1, bias_1, mlp, d_act2 = feed_forward_call(other_b, bias_of(0, 1), mlp, d_act2)
    two_c = over_two(one_c, during=(d_act2,))
    sent_b = over_cores(grads_0, grads_1)
    d_act2 = after(d_act2, *sent_b)
    *grads_0, bias_2, mlp, d_act2 = feed_forward_call(two_c, bias_of(1, 0), mlp, d_act2)
    other_c = [after(swap_cores(a), d_act2) for a in two_c]
    *grads_1, bias_3, mlp, d_act2 = feed_forward_call(other_c, bias_of(1, 1), mlp, d_act2)
    sent_c = over_cores(grads_0, grads_1)
    d_bias = [bias_0, bias_1, bias_2, bias_3]

    def cut(array, level, *earlier, during=()):
        return scatter_stage(after(array.astype(bf16), *earlier), level, levels, during)

    def grown(array):
        return array.reshape((array.shape[0],) + (2,) * levels + (own_rows, width))

    def join(pair):
        return jnp.concatenate([p.astype(bf16) for p in pair])

    sent_b, sent_c = [[grown(a) for a in part] for part in (sent_b, sent_c)]
    one_b = [cut(a, level, during=(d_act2,)) for a, level in zip(sent_b, (last, before))]
    output = relative(mlp)

    small = ((8, model), f32)
    d_resid, d_mixed, g_out, sums = call(
        residual_backward,
        [wide, wide_b, ((2, model, width), bf16), small],
        d_act2, resid, upstream, vec, mixed, own_vo, other_vo,
    )
    d_mixed, *sent_c = tie(d_mixed, *sent_c)
    dq, dk, dv, core_sums = call(
        attention_backward,
        [wide_b, wide_b, wide_b, small],
        query, key, value, d_mixed,
    )
    g_qk, g_v = call(
        attention_weight_grads,
        [((2, 2, model, width), bf16), ((2, model, width), bf16)],
        after(act1, *one_b), dq, dk, dv,
    )
    grad_rel, first_sums = call(
        input_backward,
        [wide, small],
        after(tokens, g_qk), vec, d_resid, dq, dk, dv, own_qk, other_qk, own_vo, other_vo,
    )
    g_vo = jnp.stack([g_v, g_out], axis=1)
    sent_a = over_cores((g_qk[0], g_vo[0]), (g_qk[1], g_vo[1]))
    sent_a = [grown(a) for a in sent_a]
    one_c = [cut(a, level, during=(dq,)) for a, level in zip(sent_c, (last, before))]
    two_b = [cut(a, level, during=(dq,)) for a, level in zip(one_b, (before, last))]
    one_a = [cut(a, level) for a, level in zip(sent_a, (last, before))]
    two_c = [cut(a, level, *sent_a) for a, level in zip(one_c, (before, last))]
    z_b = cut(join(two_b), z_levels[-1], *sent_a)
    two_a = [cut(a, level, *two_b) for a, level in zip(one_a, (before, last))]
    for level in z_levels[-2::-1]:
        z_b = cut(z_b, level, *one_a)
    z_c = cut(join(two_c), z_levels[-1], z_b)
    z_a = cut(join(two_a), z_levels[-1], z_c)
    z_a, first_sums = tie(z_a, first_sums)
    for level in z_levels[-2::-1]:
        z_c = cut(z_c, level)
    for level in z_levels[-2::-1]:
        z_a = cut(z_a, level, z_c)
    rows_a, rows_b, rows_c = [a.reshape(2 * half, own_rows, width) for a in (z_a, z_b, z_c)]
    input_gradient = relative(grad_rel)

    row_sums = relative(jnp.concatenate([first_sums[:2], sums[:4]]))
    hidden_sums = jnp.concatenate(
        [
            jnp.concatenate([d_bias[2 * j][:, 0], d_bias[2 * j + 1][:, 0]], axis=-1)
            for j in range(2)
        ]
    )
    half_sums = halves(jnp.concatenate([core_sums[:2], hidden_sums]))
    vec_part = jnp.concatenate(
        [row_sums[:2], half_sums[:2], row_sums[2:5], half_sums[2:], row_sums[5:]]
    )

    def add_rounds(values, *bits):
        came = [exchange(values, k, owners) for k in bits]
        values = values + came[0]
        if len(bits) == 3:
            values = values + (came[1] + came[2])
        return values

    grad_rows = jnp.concatenate(
        [rows_a, rows_b[:half], rows_c[:half], rows_b[half:], rows_c[half:]]
    )
    new_momentum = momentum_rate * momentum + grad_rows
    outgoing = new_momentum.astype(bf16)
    outgoing = jnp.concatenate([outgoing] * (owners // blocks) + [outgoing[: owners % blocks]])
    whole_slab = lax.all_to_all(
        outgoing, "dp", split_axis=0, concat_axis=0, tiled=True
    ).reshape(model, width)
    vector_grad = vec_part + swap_cores(vec_part)
    whole_slab, vector_grad = tie(whole_slab, vector_grad)
    ortho = call(newton_schulz, [((model, width), bf16)], whole_slab)[0]
    for k in range(0, levels - 1, 2):
        vector_grad = add_rounds(vector_grad, 1 << k, 2 << k, 3 << k)
    if levels % 2:
        vector_grad = add_rounds(vector_grad, 1 << (levels - 1))
    returned = lax.all_to_all(
        ortho.reshape(owners, own_rows, width),
        "dp",
        split_axis=0,
        concat_axis=0,
        tiled=True,
    ).astype(f32)[:blocks]
    new_weights = (
        weights * (1.0 - muon_rate * muon_decay) - muon_rate * 0.2 * math.sqrt(model) * returned
    )
    new_adam_first = beta_first * adam_first + (1.0 - beta_first) * vector_grad
    new_adam_second = beta_second * adam_second + (1.0 - beta_second) * vector_grad * vector_grad
    new_vectors = vectors - adam_rate * (new_adam_first / bias_first) / (
        jnp.sqrt(new_adam_second / bias_second) + adam_eps
    )
    return (
        output,
        input_gradient,
        grad_rows,
        new_weights,
        new_momentum,
        vector_grad,
        new_vectors,
        new_adam_first,
        new_adam_second,
    )


def solution(mesh):
    return jax.shard_map(
        shards,
        mesh=mesh,
        in_specs=(
            P(("dp", "tensor"), None),
            P(None, "dp", "tensor"),
            P(),
            P(None, "dp", "tensor"),
            P(),
            P(),
            P(("dp", "tensor"), None),
        ),
        out_specs=(
            P(("dp", "tensor"), None),
            P(("dp", "tensor"), None),
            P(None, "dp", "tensor"),
            P(None, "dp", "tensor"),
            P(None, "dp", "tensor"),
            P(),
            P(),
            P(),
            P(),
        ),
        check_vma=False,
    )
```

```python
import math

import jax
import jax.numpy as jnp
from jax import lax
from jax.experimental import pallas as pl
from jax.experimental.pallas import tpu as pltpu
from jax.sharding import PartitionSpec as P

HDIM = 64
SEQ = 197
NS_STEPS = 5


eps_norm = 1e-06
momentum_rate = 0.95
muon_rate = 0.1
muon_decay = 0.1
ns_first = 3.4445
ns_second = -4.775
ns_third = 2.0315
adam_rate = 0.1
beta_first = 0.9
beta_second = 0.95
bias_first = 0.19
bias_second = 0.0975
adam_eps = 1e-08
root_half = 0.7071067811865476
inv_root_pi = 0.3989422804014327

f32 = jnp.float32
bf16 = jnp.bfloat16


def layer_normalize(values, gain_row, shift_row):
    centre = values - jnp.mean(values, axis=-1, keepdims=True)
    inverse_std = lax.rsqrt(jnp.mean(centre * centre, axis=-1, keepdims=True) + eps_norm)
    normed = centre * inverse_std
    return (normed * gain_row + shift_row, normed, inverse_std)


def norm_backward_pass(upstream_gradient, gain_row, normed, inverse_std):
    scaled = upstream_gradient * gain_row
    return inverse_std * (
        scaled
        - jnp.mean(scaled, axis=-1, keepdims=True)
        - normed * jnp.mean(scaled * normed, axis=-1, keepdims=True)
    )


def gelu_value(preact):
    return 0.5 * preact * (1.0 + lax.erf(preact * root_half))


def gelu_slope(preact):
    return (
        0.5 * (1.0 + lax.erf(preact * root_half))
        + preact * jnp.exp(-0.5 * preact * preact) * inv_root_pi
    )


def exchange(array, bit, owners):
    return lax.ppermute(array, "dp", [(i, i ^ bit) for i in range(owners)])


def swap_cores(array):
    return lax.ppermute(array, "tensor", [(0, 1), (1, 0)])


def gather_stage(array, level, levels, during=()):
    other = after(exchange(array, 1 << (levels - 1 - level), 1 << levels), *during)
    return jnp.concatenate([array, other], axis=1 + level)


def scatter_stage(array, level, levels, during=()):
    axis = 1 + level
    mine = lax.slice_in_dim(array, 0, 1, axis=axis)
    theirs = lax.slice_in_dim(array, 1, 2, axis=axis)
    came = after(exchange(theirs, 1 << (levels - 1 - level), 1 << levels), *during)
    return mine.astype(f32) + came.astype(f32)


def tie(*arrays):
    return lax.optimization_barrier(arrays)


def after(array, *earlier):
    return lax.optimization_barrier((array,) + earlier)[0] if earlier else array


NN, NT, TN = ((1,), (0,)), ((1,), (1,)), ((0,), (0,))


def dot(left, right, contract=NN):
    return lax.dot_general(left, right, (contract, ((), ())), preferred_element_type=f32)


def params():
    return pltpu.CompilerParams(vmem_limit_bytes=48 * 1024 * 1024)


def column_sum(array):
    return jnp.sum(array, axis=0, keepdims=True)


def softmax_rows(query, key):
    score = dot(query, key, NT) * (HDIM ** (-0.5))
    expo = jnp.exp(score - jnp.max(score, axis=-1, keepdims=True))
    return expo / jnp.sum(expo, axis=-1, keepdims=True)


def attention_forward(
    tokens, vec, core_vec, own_qk, other_qk, own_vo, other_vo,
    act1_out, query_out, key_out, value_out, mixed_out, resid_out, act2_out,
):
    model = tokens.shape[1]
    width = own_qk.shape[2]
    act1 = layer_normalize(tokens[...], vec[0:1], vec[1:2])[0].astype(bf16)
    act1_out[...] = act1
    for k, (qk, vo) in enumerate(((own_qk, own_vo), (other_qk, other_vo))):
        cols = slice(k * width, (k + 1) * width)
        query_out[:, cols] = (dot(act1, qk[0]) + core_vec[2:3, cols]).astype(bf16)
        key_out[:, cols] = dot(act1, qk[1]).astype(bf16)
        value_out[:, cols] = (dot(act1, vo[0]) + core_vec[3:4, cols]).astype(bf16)
    for pair in range(model // (2 * HDIM)):
        lanes = slice(2 * pair * HDIM, 2 * (pair + 1) * HDIM)
        query, key, value = query_out[:, lanes], key_out[:, lanes], value_out[:, lanes]
        parts = []
        for k in range(2):
            head = slice(k * HDIM, (k + 1) * HDIM)
            prob = softmax_rows(query[:, head], key[:, head]).astype(bf16)
            parts.append(dot(prob, value[:, head]))
        mixed_out[:, lanes] = jnp.concatenate(parts, axis=1).astype(bf16)
    resid = (
        tokens[...]
        + (dot(mixed_out[:, :width], own_vo[1], NT) + dot(mixed_out[:, width:], other_vo[1], NT))
        + vec[4:5]
    )
    resid_out[...] = resid
    act2_out[...] = layer_normalize(resid, vec[5:6], vec[6:7])[0].astype(bf16)


def feed_forward(
    act2, up, first, second, bias, mlp_in, d_act2_in,
    g_first, g_second, d_bias, mlp, d_act2,
):
    @pl.when(pl.program_id(0) == 0)
    def _():
        mlp[...] = mlp_in[...]
        d_act2[...] = d_act2_in[...]

    pre = dot(act2[...], first[0]) + bias[0]
    both = 1.0 + lax.erf(pre * root_half)
    hidden = (0.5 * pre * both).astype(bf16)
    slope = 0.5 * both + pre * jnp.exp(-0.5 * pre * pre) * inv_root_pi
    mlp[...] += dot(hidden, second[0], NT)
    g_second[0] = dot(up[...], hidden, TN).astype(bf16)
    d_pre = dot(up[...], second[0]) * slope
    d_bias[0] = column_sum(d_pre)
    d_pre_b = d_pre.astype(bf16)
    g_first[0] = dot(act2[...], d_pre_b, TN).astype(bf16)
    d_act2[...] += dot(d_pre_b, first[0], NT)


def residual_backward(
    d_act2_in, resid, upstream, vec, mixed, own_vo, other_vo, d_resid_out, d_mixed_out, g_out, sums
):
    model = resid.shape[1]
    width = own_vo.shape[2]
    d_act2 = d_act2_in[...]
    _, xhat2, inv2 = layer_normalize(resid[...], vec[5:6], vec[6:7])
    d_resid = upstream[...] + norm_backward_pass(d_act2, vec[5:6], xhat2, inv2)
    d_resid_out[...] = d_resid
    sums[0:1] = column_sum(d_resid)
    sums[1:2] = column_sum(d_act2 * xhat2)
    sums[2:3] = column_sum(d_act2)
    sums[3:4] = column_sum(upstream[...])
    sums[4:8] = jnp.zeros((4, model), f32)
    d_resid_b = d_resid.astype(bf16)
    for k, vo in enumerate((own_vo, other_vo)):
        cols = slice(k * width, (k + 1) * width)
        g_out[k] = dot(d_resid_b, mixed[:, cols], TN).astype(bf16)
        d_mixed_out[:, cols] = dot(d_resid_b, vo[1]).astype(bf16)


def attention_backward(query_in, key_in, value_in, d_mixed_in, dq_out, dk_out, dv_out, core_sums):
    model = query_in.shape[1]
    for pair in range(model // (2 * HDIM)):
        lanes = slice(2 * pair * HDIM, 2 * (pair + 1) * HDIM)
        query, key, value, d_mixed = query_in[:, lanes], key_in[:, lanes], value_in[:, lanes], d_mixed_in[:, lanes]
        d_query, d_key, d_value = [], [], []
        for k in range(2):
            head = slice(k * HDIM, (k + 1) * HDIM)
            q, ky, v, dm = query[:, head], key[:, head], value[:, head], d_mixed[:, head]
            prob = softmax_rows(q, ky)
            d_prob = dot(dm, v, NT)
            delta = jnp.sum(prob * d_prob, axis=-1, keepdims=True)
            d_score = (prob * (d_prob - delta) * (HDIM ** (-0.5))).astype(bf16)
            d_value.append(dot(prob.astype(bf16), dm, TN))
            d_query.append(dot(d_score, ky))
            d_key.append(dot(d_score, q, TN))
        d_query, d_key, d_value = [jnp.concatenate(d, axis=1) for d in (d_query, d_key, d_value)]
        core_sums[0:1, lanes] = column_sum(d_query)
        core_sums[1:2, lanes] = column_sum(d_value)
        dq_out[:, lanes] = d_query.astype(bf16)
        dk_out[:, lanes] = d_key.astype(bf16)
        dv_out[:, lanes] = d_value.astype(bf16)
    core_sums[2:8] = jnp.zeros((6, model), f32)


def attention_weight_grads(act1, dq, dk, dv, g_qk, g_v):
    for k in range(2):
        cols = slice(k * g_v.shape[2], (k + 1) * g_v.shape[2])
        g_qk[k, 0] = dot(act1[...], dq[:, cols], TN).astype(bf16)
        g_qk[k, 1] = dot(act1[...], dk[:, cols], TN).astype(bf16)
        g_v[k] = dot(act1[...], dv[:, cols], TN).astype(bf16)


def input_backward(tokens, vec, d_resid, dq, dk, dv, own_qk, other_qk, own_vo, other_vo, grad, sums):
    model = tokens.shape[1]
    width = own_qk.shape[2]
    d_act1 = jnp.zeros(tokens.shape, f32)
    for k, (qk, vo) in enumerate(((own_qk, own_vo), (other_qk, other_vo))):
        cols = slice(k * width, (k + 1) * width)
        d_act1 += dot(dq[:, cols], qk[0], NT)
        d_act1 += dot(dk[:, cols], qk[1], NT)
        d_act1 += dot(dv[:, cols], vo[0], NT)
    _, xhat1, inv1 = layer_normalize(tokens[...], vec[0:1], vec[1:2])
    grad[...] = d_resid[...] + norm_backward_pass(d_act1, vec[0:1], xhat1, inv1)
    sums[0:1] = column_sum(d_act1 * xhat1)
    sums[1:2] = column_sum(d_act1)
    sums[2:8] = jnp.zeros((6, model), f32)


def halve(array):
    high = array.astype(bf16)
    return high, (array - high.astype(f32)).astype(bf16)


def newton_schulz(slab, out):
    values = slab[...].astype(f32)
    current = values / (jnp.sqrt(jnp.sum(values * values)) + 1e-07)
    width = values.shape[1]
    for turn in range(NS_STEPS):
        high, low = halve(current)
        product = dot(high, jnp.concatenate([high, low], axis=1), TN)
        mixed = product[:, width:]
        gram = product[:, :width] + (mixed + mixed.T)
        gram_high, gram_low = halve(gram)
        product = dot(gram_high, jnp.concatenate([gram_high, gram_low], axis=1))
        mixed = product[:, width:]
        square = product[:, :width] + (mixed + mixed.T)
        poly = ns_second * gram + ns_third * square
        if turn == NS_STEPS - 1:
            rows = lax.broadcasted_iota(jnp.int32, poly.shape, 0)
            columns = lax.broadcasted_iota(jnp.int32, poly.shape, 1)
            factor = poly + jnp.where(rows == columns, ns_first, 0.0)
            out[...] = dot(high, factor.astype(bf16)).astype(bf16)
            break
        poly_high, poly_low = halve(poly)
        product = dot(high, jnp.concatenate([poly_high, poly_low], axis=1))
        current = ns_first * current + (
            product[:, :width] + (product[:, width:] + dot(low, poly_high))
        )


def call(kernel, outs, *args):
    return pl.pallas_call(
        kernel,
        out_shape=[jax.ShapeDtypeStruct(s, d) for s, d in outs],
        compiler_params=params(),
    )(*args)


def shards(
    block_input_tokens, weights, vectors, momentum, adam_first, adam_second, output_gradient
):
    owners = lax.axis_size("dp")
    levels = owners.bit_length() - 1
    blocks, own_rows, width = weights.shape
    seq, model = block_input_tokens.shape
    count = (blocks - 4) // 2
    half = count // 2
    here = lax.axis_index("dp")
    core = lax.axis_index("tensor")

    feature = jnp.arange(model)
    source = ((feature // own_rows) ^ here) * own_rows + feature % own_rows
    reorder = (feature[:, None] == source[None, :]).astype(f32)

    def relative(array):
        return jnp.dot(array, reorder, precision=lax.Precision.HIGHEST)

    def halves(row):
        return jnp.where(core == 0, row, jnp.concatenate([row[..., width:], row[..., :width]], -1))

    cast = weights.astype(bf16)
    last, before = levels - 1, levels - 2
    z_levels = list(range(levels - 2))

    def stage(array, level, *earlier, during=()):
        return gather_stage(after(array, *earlier), level, levels, during)

    def whole(array):
        return array.reshape(array.shape[0], own_rows << levels, width)

    def chunk(*starts):
        array = jnp.concatenate([cast[i : i + half] for i in starts])
        return array.reshape((2 * half,) + (1,) * levels + (own_rows, width))

    def over_z(array, first_after, then_after):
        array = stage(array, z_levels[0], *first_after)
        first = array
        for level in z_levels[1:]:
            array = stage(array, level, *then_after)
            then_after = ()
        return first, array

    def over_one(array, *earlier):
        return [
            stage(array[half * k : half * (k + 1)], level, *earlier)
            for k, level in ((0, before), (1, last))
        ]

    def over_two(pair, *earlier, during=()):
        return [
            whole(stage(one, level, *earlier, during=during))
            for one, level in zip(pair, (last, before))
        ]

    first_a, z_a = over_z(chunk(0, 2), (), ())
    first_b, z_b = over_z(chunk(4, 4 + count), (first_a,), ())
    one_a = over_one(z_a, first_b)
    first_c, z_c = over_z(chunk(4 + half, 4 + count + half), (first_b,), ())
    own_qk, own_vo = over_two(one_a)
    one_b = over_one(z_b, first_c, *one_a)
    other_qk, other_vo = [swap_cores(a) for a in (own_qk, own_vo)]
    one_c = over_one(z_c, *one_b)

    moved = relative(jnp.concatenate([block_input_tokens, output_gradient, vectors]))
    tokens, upstream, vec = moved[:seq], moved[seq : 2 * seq], moved[2 * seq :]
    core_vec = halves(vectors)
    up_b = upstream.astype(bf16)

    wide, wide_b = ((seq, model), f32), ((seq, model), bf16)
    act1, query, key, value, mixed, resid, act2 = call(
        attention_forward,
        [wide_b] * 5 + [wide, wide_b],
        tokens, vec, core_vec, own_qk, other_qk, own_vo, other_vo,
    )

    two_b = over_two(one_b, z_c, during=(act1,))
    other_b = [swap_cores(after(a, *one_c)) for a in two_b]

    mlp = resid + vec[7 + count]
    d_act2 = jnp.zeros((seq, model), f32)

    def feed_forward_call(weights_pair, bias, mlp, d_act2):
        whole = pl.BlockSpec((seq, model), lambda k: (0, 0))
        block = pl.BlockSpec((1, model, width), lambda k: (k, 0, 0))
        row = pl.BlockSpec((1, 1, width), lambda k: (k, 0, 0))
        grads = jax.ShapeDtypeStruct((half, model, width), bf16)
        total = jax.ShapeDtypeStruct((seq, model), f32)
        return pl.pallas_call(
            feed_forward,
            grid=(half,),
            in_specs=[whole, whole, block, block, row, whole, whole],
            out_specs=[block, block, row, whole, whole],
            out_shape=[grads, grads, jax.ShapeDtypeStruct((half, 1, width), f32), total, total],
            compiler_params=params(),
        )(act2, up_b, *weights_pair, bias, mlp, d_act2)

    bias_hidden = core_vec[7 : 7 + count].reshape(count, 1, 2, width)
    def bias_of(j, k):
        return bias_hidden[j * half : (j + 1) * half, :, k]

    def over_cores(own, other, *during):
        return [
            (g.astype(f32) + after(swap_cores(o), *during).astype(f32)).astype(bf16)
            for g, o in zip(own, other)
        ]

    *grads_0, bias_0, mlp, d_act2 = feed_forward_call(two_b, bias_of(0, 0), mlp, after(d_act2, *one_c))
    other_b = [after(a, d_act2) for a in other_b]
    *grads_1, bias_1, mlp, d_act2 = feed_forward_call(other_b, bias_of(0, 1), mlp, d_act2)
    two_c = over_two(one_c, during=(d_act2,))
    sent_b = over_cores(grads_0, grads_1)
    d_act2 = after(d_act2, *sent_b)
    *grads_0, bias_2, mlp, d_act2 = feed_forward_call(two_c, bias_of(1, 0), mlp, d_act2)
    other_c = [after(swap_cores(a), d_act2) for a in two_c]
    *grads_1, bias_3, mlp, d_act2 = feed_forward_call(other_c, bias_of(1, 1), mlp, d_act2)
    sent_c = over_cores(grads_0, grads_1)
    d_bias = [bias_0, bias_1, bias_2, bias_3]

    def cut(array, level, *earlier, during=()):
        return scatter_stage(after(array.astype(bf16), *earlier), level, levels, during)

    def grown(array):
        return array.reshape((array.shape[0],) + (2,) * levels + (own_rows, width))

    def join(pair):
        return jnp.concatenate([p.astype(bf16) for p in pair])

    sent_b, sent_c = [[grown(a) for a in part] for part in (sent_b, sent_c)]
    one_b = [cut(a, level, during=(d_act2,)) for a, level in zip(sent_b, (last, before))]
    output = relative(mlp)

    small = ((8, model), f32)
    d_resid, d_mixed, g_out, sums = call(
        residual_backward,
        [wide, wide_b, ((2, model, width), bf16), small],
        d_act2, resid, upstream, vec, mixed, own_vo, other_vo,
    )
    d_mixed, *sent_c = tie(d_mixed, *sent_c)
    dq, dk, dv, core_sums = call(
        attention_backward,
        [wide_b, wide_b, wide_b, small],
        query, key, value, d_mixed,
    )
    g_qk, g_v = call(
        attention_weight_grads,
        [((2, 2, model, width), bf16), ((2, model, width), bf16)],
        after(act1, *one_b), dq, dk, dv,
    )
    grad_rel, first_sums = call(
        input_backward,
        [wide, small],
        after(tokens, g_qk), vec, d_resid, dq, dk, dv, own_qk, other_qk, own_vo, other_vo,
    )
    g_vo = jnp.stack([g_v, g_out], axis=1)
    sent_a = over_cores((g_qk[0], g_vo[0]), (g_qk[1], g_vo[1]))
    sent_a = [grown(a) for a in sent_a]
    one_c = [cut(a, level, during=(dq,)) for a, level in zip(sent_c, (last, before))]
    two_b = [cut(a, level, during=(dq,)) for a, level in zip(one_b, (before, last))]
    one_a = [cut(a, level) for a, level in zip(sent_a, (last, before))]
    two_c = [cut(a, level, *sent_a) for a, level in zip(one_c, (before, last))]
    z_b = cut(join(two_b), z_levels[-1], *sent_a)
    two_a = [cut(a, level, *two_b) for a, level in zip(one_a, (before, last))]
    for level in z_levels[-2::-1]:
        z_b = cut(z_b, level, *one_a)
    z_c = cut(join(two_c), z_levels[-1], z_b)
    z_a = cut(join(two_a), z_levels[-1], z_c)
    z_a, first_sums = tie(z_a, first_sums)
    for level in z_levels[-2::-1]:
        z_c = cut(z_c, level)
    for level in z_levels[-2::-1]:
        z_a = cut(z_a, level, z_c)
    rows_a, rows_b, rows_c = [a.reshape(2 * half, own_rows, width) for a in (z_a, z_b, z_c)]
    input_gradient = relative(grad_rel)

    row_sums = relative(jnp.concatenate([first_sums[:2], sums[:4]]))
    hidden_sums = jnp.concatenate(
        [
            jnp.concatenate([d_bias[2 * j][:, 0], d_bias[2 * j + 1][:, 0]], axis=-1)
            for j in range(2)
        ]
    )
    half_sums = halves(jnp.concatenate([core_sums[:2], hidden_sums]))
    vec_part = jnp.concatenate(
        [row_sums[:2], half_sums[:2], row_sums[2:5], half_sums[2:], row_sums[5:]]
    )

    def add_rounds(values, *bits):
        came = [exchange(values, k, owners) for k in bits]
        values = values + came[0]
        if len(bits) == 3:
            values = values + (came[1] + came[2])
        return values

    grad_rows = jnp.concatenate(
        [rows_a, rows_b[:half], rows_c[:half], rows_b[half:], rows_c[half:]]
    )
    new_momentum = momentum_rate * momentum + grad_rows
    outgoing = new_momentum.astype(bf16)
    outgoing = jnp.concatenate([outgoing] * (owners // blocks) + [outgoing[: owners % blocks]])
    whole_slab = lax.all_to_all(
        outgoing, "dp", split_axis=0, concat_axis=0, tiled=True
    ).reshape(model, width)
    vector_grad = vec_part + swap_cores(vec_part)
    whole_slab, vector_grad = tie(whole_slab, vector_grad)
    ortho = call(newton_schulz, [((model, width), bf16)], whole_slab)[0]
    for k in range(0, levels - 1, 2):
        vector_grad = add_rounds(vector_grad, 1 << k, 2 << k, 3 << k)
    if levels % 2:
        vector_grad = add_rounds(vector_grad, 1 << (levels - 1))
    returned = lax.all_to_all(
        ortho.reshape(owners, own_rows, width),
        "dp",
        split_axis=0,
        concat_axis=0,
        tiled=True,
    ).astype(f32)[:blocks]
    new_weights = (
        weights * (1.0 - muon_rate * muon_decay) - muon_rate * 0.2 * math.sqrt(model) * returned
    )
    new_adam_first = beta_first * adam_first + (1.0 - beta_first) * vector_grad
    new_adam_second = beta_second * adam_second + (1.0 - beta_second) * vector_grad * vector_grad
    new_vectors = vectors - adam_rate * (new_adam_first / bias_first) / (
        jnp.sqrt(new_adam_second / bias_second) + adam_eps
    )
    return (
        output,
        input_gradient,
        grad_rows,
        new_weights,
        new_momentum,
        vector_grad,
        new_vectors,
        new_adam_first,
        new_adam_second,
    )


def solution(mesh):
    return jax.shard_map(
        shards,
        mesh=mesh,
        in_specs=(
            P(("dp", "tensor"), None),
            P(None, "dp", "tensor"),
            P(),
            P(None, "dp", "tensor"),
            P(),
            P(),
            P(("dp", "tensor"), None),
        ),
        out_specs=(
            P(("dp", "tensor"), None),
            P(("dp", "tensor"), None),
            P(None, "dp", "tensor"),
            P(None, "dp", "tensor"),
            P(None, "dp", "tensor"),
            P(),
            P(),
            P(),
            P(),
        ),
        check_vma=False,
    )
```
